256 devices in a mesh: dp: 32 (over x_lo, z, core), mp: 8 (over y, x_hi).
Axes of the slice: x: 4 (x_hi: 2, x_lo: 2; x = x_hi * 2 + x_lo), y: 4, z: 8, core: 2. Of those that a mesh axis runs over, the one named last changes fastest.
Arguments:
- student_feats: bfloat16 [96, 112, 1408], P('dp'), may hold values from -7 to 7
- keep_index: int32 [96, 112], P('dp'), may hold values from 0 to 559, as said below
- hidden_six: bfloat16 [96, 560, 12800], P('dp', None, 'mp'), may hold values from -6 to 6
- resid_six: bfloat16 [96, 560, 3200], P('dp', None, 'mp'), may hold values from -32 to 32
- down_six: bfloat16 [12800, 3200], P('mp', 'dp'), may hold values from -0.0546875 to 0.0546875
- hidden_giant: bfloat16 [96, 560, 6144], P('dp', None, 'mp'), may hold values from -6 to 6
- resid_giant: bfloat16 [96, 560, 1408], P('dp', None, 'mp'), may hold values from -32 to 32
- down_giant: bfloat16 [6144, 1408], P('mp', 'dp'), may hold values from -0.078125 to 0.078125
- proj_six: bfloat16 [1408, 3200], P(None, 'mp'), may hold values from -5 to 5
- proj_giant: bfloat16 [1408, 1408], P(None, 'mp'), may hold values from -5 to 5
Outputs:
- grad_student: float32 [96, 112, 1408], P('dp', None, 'mp')
- grad_proj_six: float32 [1408, 3200], P(None, 'mp')
- grad_proj_giant: float32 [1408, 1408], P(None, 'mp')
- loss: float32 [], replicated
The draws below stay inside these ranges and needn't reach their ends.
Inputs may be any that keep to these rules, and one draw needn't show every extreme that they name: `keep_index`: each row holds 112 distinct positions of the clip's tokens in rising order.
All inputs are finite; a program needn't handle non-finite values.
Results may differ from the reference program's by a relative error of at most 0.015.
Values may be sent and summed in bfloat16 or wider, within the bound.
A program may use at most 128 MiB of HBM per device.

```python
import math
import jax
import jax.numpy as jnp
from jax import lax

DS = 1408
D6 = 3200
FF6 = 12800
DG = 1408
FFG = 6144
CLIP_LEN = 560
KEEP = 112
CLIPS = 96
N_MP = 8


def kept_positions(key):
    key = jax.random.fold_in(key, 7)
    clip_keys = jax.random.split(key, CLIPS)

    def one_clip(clip_key):
        shuffled = jax.random.permutation(clip_key, CLIP_LEN)
        return jnp.sort(shuffled[:KEEP])
    return jax.vmap(one_clip)(clip_keys).astype(jnp.int32)


def shared_field(key):
    key = jax.random.fold_in(key, 11)
    return jax.random.truncated_normal(key, -5.0, 5.0, (CLIPS, CLIP_LEN, DS), jnp.float32)


def token_strength(key, lowest, highest):
    key = jax.random.fold_in(key, 13)
    clip_key, token_key = jax.random.split(key)
    clip_level = jnp.exp(jax.random.uniform(clip_key, (CLIPS, 1), jnp.float32, math.log(lowest), math.log(highest)))
    token_level = jnp.exp(jax.random.uniform(token_key, (CLIPS, CLIP_LEN), jnp.float32, math.log(0.5), math.log(2.0)))
    return clip_level * token_level


def spread_field(key, width, lowest, highest):
    base = shared_field(key)
    columns = jnp.arange(width) % DS
    strength = token_strength(key, lowest, highest)
    return jnp.take(base, columns, axis=2) * strength[:, :, None]


def head_matrix(key, noise, width):
    gain = 3.0 * jax.random.uniform(key, (1, width), jnp.float32, 0.8, 1.2)
    match = jnp.arange(width)[None, :] % DS == jnp.arange(DS)[:, None]
    return (noise / math.sqrt(DS) + jnp.where(match, gain, 0.0)).astype(jnp.bfloat16)


def draw_keep_index(key, part):
    return kept_positions(key)


def draw_student_feats(key, part):
    base = shared_field(key)
    kept = kept_positions(key)
    chosen = jnp.take_along_axis(base, kept[:, :, None], axis=1)
    key = jax.random.fold_in(key, 21)
    noise = jax.random.truncated_normal(key, -5.0, 5.0, (CLIPS, KEEP, DS), jnp.float32)
    return (0.95 * chosen + 0.3 * noise).astype(jnp.bfloat16)


def draw_resid_six(key, part):
    common = spread_field(key, D6, 0.3, 3.0)
    key = jax.random.fold_in(key, 41)
    noise = jax.random.truncated_normal(key, -5.0, 5.0, (CLIPS, CLIP_LEN, D6), jnp.float32)
    return (common + 0.3 * noise).astype(jnp.bfloat16)


def draw_resid_giant(key, part):
    common = spread_field(key, DG, 0.3, 3.0)
    key = jax.random.fold_in(key, 43)
    noise = jax.random.truncated_normal(key, -5.0, 5.0, (CLIPS, CLIP_LEN, DG), jnp.float32)
    return (common + 0.3 * noise).astype(jnp.bfloat16)


def draw_proj_six(key, part):
    key = jax.random.fold_in(key, 31)
    noise_key, gain_key = jax.random.split(key)
    noise = jax.random.truncated_normal(noise_key, -5.0, 5.0, (DS, D6), jnp.float32)
    return head_matrix(gain_key, noise, D6)


def draw_proj_giant(key, part):
    key = jax.random.fold_in(key, 33)
    noise_key, gain_key = jax.random.split(key)
    noise = jax.random.truncated_normal(noise_key, -5.0, 5.0, (DS, DG), jnp.float32)
    return head_matrix(gain_key, noise, DG)


def level_of(stream_key, shape, pieces, least, largest):
    level = 1.0
    for dim, shards_of in pieces:
        heights = jax.random.uniform(jax.random.fold_in(jax.random.fold_in(stream_key, 6), dim), (shards_of,), jnp.float32, least / len(pieces), largest / len(pieces))
        level = level * jnp.repeat(jnp.exp(heights), shape[dim] // shards_of).reshape((-1,) + (1,) * (len(shape) - 1 - dim))
    return level


def scatter_about(stream_key, dims, scale, bound, pieces=(), dtype=jnp.bfloat16):
    array = scale * jax.random.normal(stream_key, dims, jnp.float32)
    if pieces:
        array = array * level_of(stream_key, dims, pieces, -0.22, 0.18)
    return jnp.clip(array, -bound, bound).astype(dtype)


def setup_inputs(seed: int = 0) -> dict:
    arg_keys = jax.random.split(jax.random.key(seed), 11)
    student_feats = draw_student_feats(jax.random.fold_in(arg_keys[10], 71), 0)
    keep_index = draw_keep_index(jax.random.fold_in(arg_keys[10], 71), 0)
    hidden_six = scatter_about(arg_keys[2], (CLIPS, CLIP_LEN, FF6), 1.0, 6.0, ((0, 32), (2, 8)))
    resid_six = draw_resid_six(jax.random.fold_in(arg_keys[10], 71), 0)
    down_six = scatter_about(arg_keys[4], (FF6, D6), FF6 ** -0.5, 0.0546875, ((0, 8), (1, 32)))
    hidden_giant = scatter_about(arg_keys[5], (CLIPS, CLIP_LEN, FFG), 1.0, 6.0, ((0, 32), (2, 8)))
    resid_giant = draw_resid_giant(jax.random.fold_in(arg_keys[10], 71), 0)
    down_giant = scatter_about(arg_keys[7], (FFG, DG), FFG ** -0.5, 0.078125, ((0, 8), (1, 32)))
    proj_six = draw_proj_six(jax.random.fold_in(arg_keys[10], 71), 0)
    proj_giant = draw_proj_giant(jax.random.fold_in(arg_keys[10], 71), 0)
    return dict(student_feats=student_feats, keep_index=keep_index, hidden_six=hidden_six, resid_six=resid_six, down_six=down_six, hidden_giant=hidden_giant, resid_giant=resid_giant, down_giant=down_giant, proj_six=proj_six, proj_giant=proj_giant)


loss_scale = 256.0
head_scale = 64.0
norm_eps = 1e-06

def block_sums(rows, down):
    row_count = rows.shape[0]
    row_blocks = rows.reshape(row_count, N_MP, -1).transpose(1, 0, 2)
    weight_blocks = down.reshape(N_MP, -1, down.shape[1])

    def add_block(total, pair):
        partial_sum = jnp.dot(pair[0], pair[1], preferred_element_type=jnp.float32).astype(jnp.bfloat16)
        partial_sum = lax.optimization_barrier(partial_sum)
        return (total + partial_sum.astype(jnp.float32), None)
    start_total = jnp.zeros((row_count, down.shape[1]), jnp.float32)
    total, unused = lax.scan(add_block, start_total, (row_blocks, weight_blocks))
    return total

def select_kept(values, keep_index):
    chosen = jnp.take_along_axis(values, keep_index[:, :, None].astype(jnp.int32), axis=1)
    return chosen.reshape(-1, values.shape[2])

def head_branch(student_rows, target, weights):
    outputs = jnp.dot(student_rows, weights, preferred_element_type=jnp.float32)
    norm_out = jnp.sqrt(lax.optimization_barrier(jnp.sum(outputs * outputs, axis=1)) + norm_eps)
    norm_tar = jnp.sqrt(lax.optimization_barrier(jnp.sum(target * target, axis=1)) + norm_eps)
    cosine = lax.optimization_barrier(jnp.sum(outputs * target, axis=1)) / (norm_out * norm_tar)
    grad_out = -loss_scale * (target / (norm_out * norm_tar)[:, None] - (cosine / (norm_out * norm_out))[:, None] * outputs)
    grad_out = grad_out.astype(jnp.bfloat16)
    grad_weights = jnp.dot(student_rows.T, grad_out, preferred_element_type=jnp.float32)
    grad_weights = grad_weights * (head_scale / student_rows.shape[0])
    grad_rows = jnp.dot(grad_out, weights.T, preferred_element_type=jnp.float32)
    return (cosine, grad_weights, grad_rows)

def reference(student_feats, keep_index, hidden_six, resid_six, down_six, hidden_giant, resid_giant, down_giant, proj_six, proj_giant):
    target_six = block_sums(select_kept(hidden_six, keep_index), down_six) + select_kept(resid_six, keep_index).astype(jnp.float32)
    target_giant = block_sums(select_kept(hidden_giant, keep_index), down_giant) + select_kept(resid_giant, keep_index).astype(jnp.float32)
    student_rows = student_feats.reshape(-1, student_feats.shape[2])
    cosine_six, grad_proj_six, back_six = head_branch(student_rows, target_six, proj_six)
    cosine_giant, grad_proj_giant, back_giant = head_branch(student_rows, target_giant, proj_giant)
    loss = jnp.mean(2.0 - cosine_six - cosine_giant)
    grad_student = (back_six + back_giant).reshape(student_feats.shape)
    return (grad_student, grad_proj_six, grad_proj_giant, loss)
```

```python
import functools

import jax
import jax.numpy as jnp
from jax import lax
from jax.experimental import pallas as pl
from jax.experimental.pallas import tpu as pltpu
from jax.sharding import PartitionSpec as P

loss_scale = 256.0
head_scale = 64.0
norm_eps = 1e-06

NZ = 8
NY = 4
F32 = jnp.float32
BF16 = jnp.bfloat16
MESH = pl.DeviceIdType.MESH

SENDS = (
    ((0, 0), (0, 0), (0, 0)),
    ((0, -1), (0, 1), (0, -1)),
    ((0, -2), (0, 2), (0, -2)),
    ((0, -3), (1, 0), (0, 3)),
    ((1, -2), (1, 1), (0, 4)),
)
RECVS = (
    ((0, -1), (0, 1), (1, 0)),
    ((0, -2), (0, 2), (1, -1)),
    ((0, -3), (0, 3), (1, -2)),
    ((0, -4), (1, 1), (1, 3)),
    ((1, -3), (1, 2), (1, 4)),
)
STEPS = len(SENDS)
OWN = 3 * STEPS
Z_ORDER = (4, 3, 5, 2, 6, 1, 7)


def nt(a, b):
    return lax.dot_general(a, b, (((1,), (1,)), ((), ())), preferred_element_type=F32)


def nn(a, b):
    return lax.dot_general(a, b, (((1,), (0,)), ((), ())), preferred_element_type=F32)


def kernel(
    token_total,
    keep_row,
    keep_col,
    stu_hbm,
    h6_hbm,
    r6_hbm,
    w6_hbm,
    hg_hbm,
    rg_hbm,
    wg_hbm,
    p6_hbm,
    pg_hbm,
    gp6_out,
    gpg_out,
    back_out,
    loss_out,
    w6_in,
    wg_in,
    gath6,
    gathg,
    h6,
    hg,
    r6,
    rg,
    rows6,
    rowsg,
    stu,
    pt,
    pmat,
    part,
    yrecv,
    xsend,
    xrecv,
    tgt,
    outs,
    stats,
    grad,
    gs,
    grecv,
    gxs,
    gxr,
    gzs,
    gzr,
    ag,
    fout,
    bsend,
    byr,
    bxs,
    bxr,
    bfin,
    lossz,
    lossx,
    lossc,
    lossv,
    load_sem,
    wsend_sem,
    wrecv_sem,
    psend_sem,
    precv_sem,
    ysend_sem,
    yrecv_sem,
    xh_sem,
    st_sem,
    g_sem,
    agz_sem,
    agx_sem,
    agp_sem,
    b_sem,
    l_sem,
    out_sem,
):
    dp = lax.axis_index("dp")
    mp = lax.axis_index("mp")
    c = dp % 2
    z = (dp // 2) % NZ
    xl = dp // (2 * NZ)
    y = mp // 2
    xh = mp % 2

    pair = {"dp": dp + 1 - 2 * c}
    xpart = {"dp": (1 - xl) * 2 * NZ + z * 2 + c}
    xhpart = {"mp": y * 2 + 1 - xh}

    def at_z(zz):
        return {"dp": xl * 2 * NZ + zz * 2 + c}

    def at_mp(m):
        return {"mp": m}

    zup = at_z((z + 1) % NZ)
    zdown = at_z((z + NZ - 1) % NZ)

    def rcopy(src, dst, ssem, rsem, device):
        return pltpu.make_async_remote_copy(
            src_ref=src, dst_ref=dst, send_sem=ssem, recv_sem=rsem, device_id=device, device_id_type=MESH
        )

    loads = [
        pltpu.make_async_copy(src, dst, load_sem.at[i])
        for i, (src, dst) in enumerate(
            (
                (w6_hbm, w6_in),
                (wg_hbm, wg_in),
                (h6_hbm, h6),
                (hg_hbm, hg),
                (stu_hbm, stu),
                (p6_hbm, pt.at[pl.ds(0, 400)]),
                (pg_hbm, pt.at[pl.ds(400, 176)]),
                (r6_hbm, r6),
                (rg_hbm, rg),
            )
        )
    ]
    for load in loads:
        load.start()

    barrier = pltpu.get_barrier_semaphore()
    peers = [pair, xpart]
    peers += [at_z((z + o) % NZ) for o in range(1, NZ)]
    peers += [at_mp((mp + o) % 8) for o in range(1, 8)]
    for device in peers:
        pl.semaphore_signal(barrier, inc=1, device_id=device, device_id_type=MESH)

    def slot_of(block):
        plane, off = block
        pl_ = xl if plane == 0 else 1 - xl
        return pl_ * 2 * NZ + ((z + off + NZ) % NZ) * 2

    own = dp
    loads[0].wait()
    loads[1].wait()
    gath6[own] = jnp.zeros((112, 1664), BF16)
    gathg[own] = jnp.zeros((48, 768), BF16)
    gath6[own, 0:100, 0:1600] = w6_in[...]
    gathg[own, 0:44, :] = wg_in[...]

    pl.semaphore_wait(barrier, len(peers))

    def piece(p, slot):
        if p == 0:
            return gath6.at[slot, pl.ds(0, 64)]
        if p == 1:
            return gath6.at[slot, pl.ds(64, 48)]
        return gathg.at[slot]

    wtargets = (zup, zdown, xpart)
    pending = []

    def send_w(s, k, p):
        ref = piece(p, slot_of(SENDS[s][k]) + c)
        cp = rcopy(ref, ref, wsend_sem.at[p, 3 * s + k], wrecv_sem.at[p, 3 * s + k], wtargets[k])
        cp.start()
        pending.append(cp)

    def send_pair(unit, block, p):
        ref = piece(p, slot_of(block) + c)
        cp = rcopy(ref, ref, psend_sem.at[p, unit], precv_sem.at[p, unit], pair)
        cp.start()
        pending.append(cp)

    def wait_w(s, k, p):
        ref = piece(p, slot_of(RECVS[s][k]) + c)
        rcopy(ref, ref, wsend_sem.at[p, 3 * s + k], wrecv_sem.at[p, 3 * s + k], wtargets[k]).wait_recv()

    for p in range(3):
        for k in range(3):
            send_w(0, k, p)
    for p in range(3):
        send_pair(OWN, (0, 0), p)

    rows6[:, 1536:1664] = jnp.zeros((336, 128), BF16)
    loads[2].wait()
    loads[3].wait()
    for i in range(3):
        lane = lax.broadcasted_iota(jnp.int32, (112, 560), 1)
        pick = (keep_col[112 * i : 112 * i + 112, :] == lane).astype(F32).astype(BF16)
        rows6[112 * i : 112 * i + 112, 0:1600] = nn(pick, h6[i]).astype(BF16)
        rowsg[112 * i : 112 * i + 112, :] = nn(pick, hg[i]).astype(BF16)

    ysends = []

    def compute(unit, block):
        slot = slot_of(block)
        for p in range(3):
            ref = piece(p, slot + 1 - c)
            rcopy(ref, ref, psend_sem.at[p, unit], precv_sem.at[p, unit], pair).wait_recv()
        w = gath6[pl.ds(slot, 2)].reshape(224, 1664)
        part[pl.ds(slot, 2), 0:112, :] = nt(w, rows6[...]).astype(BF16).reshape(2, 112, 336)
        w = gathg[pl.ds(slot, 2)].reshape(96, 768)
        part[pl.ds(slot, 2), 112:160, :] = nt(w, rowsg[...]).astype(BF16).reshape(2, 48, 336)
        to_y = slot // 8
        u = (slot // 2) % 4
        o = (y - to_y + 3) % NY
        away = to_y != y

        def descriptor():
            ref = part.at[pl.ds(slot, 2)]
            return rcopy(ref, yrecv.at[o, u], ysend_sem.at[unit], yrecv_sem.at[o, u], at_mp(to_y * 2 + xh))

        @pl.when(away)
        def _():
            descriptor().start()

        ysends.append((away, descriptor))

    def heads():
        for load in loads[4:]:
            load.wait()
        outs[...] = nt(pt[...], stu[...])
        for l in range(11):
            pmat[128 * l : 128 * l + 128, :] = pt[:, 128 * l : 128 * l + 128].T
        for i in range(3):
            pos = lax.broadcasted_iota(jnp.int32, (560, 336), 0)
            col = lax.broadcasted_iota(jnp.int32, (560, 336), 1)
            clip = (col >= 112 * i) & (col < 112 * i + 112)
            pick = ((keep_row[...] == pos) & clip).astype(F32).astype(BF16)
            a = nn(r6[i], pick)
            b = nn(rg[i], pick)
            if i == 0:
                tgt[0:400, :] = a
                tgt[400:576, :] = b
            else:
                tgt[0:400, :] += a
                tgt[400:576, :] += b

    for s in range(STEPS):
        for p in range(3):
            for k in range(3):
                wait_w(s, k, p)
            if s + 1 < STEPS:
                for k in range(3):
                    send_w(s + 1, k, p)
            for k in range(3):
                send_pair(3 * s + k, RECVS[s][k], p)
            if s == 0:
                if p == 0:
                    compute(OWN, (0, 0))
                if p == 2:
                    heads()
            else:
                compute(3 * (s - 1) + p, RECVS[s - 1][p])
    for k in range(3):
        compute(3 * (STEPS - 1) + k, RECVS[STEPS - 1][k])

    def summed(u, cc):
        slot = y * 8 + u * 2 + cc
        total = part[slot].astype(F32)
        for o in range(3):
            total = total + yrecv[o, u, cc].astype(F32)
        return total

    def wait_y(u):
        for o in range(3):
            ref = yrecv.at[o, u]
            rcopy(ref, ref, ysend_sem.at[0], yrecv_sem.at[o, u], xhpart).wait_recv()

    for k in range(2):
        u = 2 * (1 - xh) + k
        wait_y(u)
        for cc in range(2):
            xsend[k, cc] = summed(u, cc).astype(BF16)
        cp = rcopy(xsend.at[k], xrecv.at[k], xh_sem.at[0, k], xh_sem.at[1, k], xhpart)
        cp.start()
        pending.append(cp)
    for k in range(2):
        u = 2 * xh + k
        wait_y(u)
        rcopy(xsend.at[k], xrecv.at[k], xh_sem.at[0, k], xh_sem.at[1, k], xhpart).wait_recv()
        for cc in range(2):
            total = summed(u, cc) + xrecv[k, cc].astype(F32)
            f = 100 * (2 * k + cc)
            tgt[f : f + 100, :] += total[0:100]
            f = 400 + 44 * (2 * k + cc)
            tgt[f : f + 44, :] += total[112:156]

    def sums(lo, hi):
        t = tgt[lo:hi, :]
        o = outs[lo:hi, :]
        return [
            jnp.sum(o * t, axis=0, keepdims=True),
            jnp.sum(o * o, axis=0, keepdims=True),
            jnp.sum(t * t, axis=0, keepdims=True),
        ]

    for i, row in enumerate(sums(0, 400) + sums(400, 576)):
        stats[mp, i : i + 1, :] = row
    for i in range(6, 8):
        stats[mp, i : i + 1, :] = jnp.zeros((1, 336), F32)
    st = []
    for o in range(1, 8):
        m = (mp + o) % 8
        cp = rcopy(stats.at[mp], stats.at[mp], st_sem.at[0, o], st_sem.at[1, mp], at_mp(m))
        cp.start()
        pending.append(cp)
    for o in range(1, 8):
        m = (mp + o) % 8
        rcopy(stats.at[m], stats.at[m], st_sem.at[0, o], st_sem.at[1, m], at_mp(m)).wait_recv()
    total = stats[0]
    for m in range(1, 8):
        total = total + stats[m]

    def gradient(lo, hi, i):
        norm_out = jnp.sqrt(total[i + 1 : i + 2] + norm_eps)
        norm_tar = jnp.sqrt(total[i + 2 : i + 3] + norm_eps)
        both = norm_out * norm_tar
        cosine = total[i : i + 1] / both
        a = -loss_scale / both
        b = loss_scale * cosine / (norm_out * norm_out)
        grad[lo:hi, :] = (tgt[lo:hi, :] * a + outs[lo:hi, :] * b).astype(BF16)
        return cosine

    cos6 = gradient(0, 400, 0)
    cosg = gradient(400, 576, 3)
    grad[576:640, :] = jnp.zeros((64, 336), BF16)
    loss_local = jnp.sum(2.0 - cos6 - cosg, axis=1, keepdims=True)
    lossz[z] = jnp.broadcast_to(loss_local, (8, 128))
    for o in range(1, NZ):
        zz = (z + o) % NZ
        cp = rcopy(lossz.at[z], lossz.at[z], l_sem.at[0, o], l_sem.at[1, z], at_z(zz))
        cp.start()
        pending.append(cp)

    order = [(z + o) % NZ for o in Z_ORDER] + [z]
    for kk in order:
        rows = grad[pl.ds(pl.multiple_of(kk * 80, 16), 80), :]
        g = nn(rows, stu[...]).astype(BF16)
        for q in range(3):
            gs[kk, q] = g[:, 384 * q : 384 * q + 384]
        gs[kk, 3, :, 0:256] = g[:, 1152:1408]
        gs[kk, 3, :, 256:384] = jnp.zeros((80, 128), BF16)
        cp = rcopy(gs.at[kk, pl.ds(2 * (1 - c), 2)], grecv.at[kk], g_sem.at[0, kk], g_sem.at[1, kk], pair)
        cp.start()
        pending.append(cp)

    for kk in order:
        rcopy(grecv.at[kk], grecv.at[kk], g_sem.at[0, kk], g_sem.at[1, kk], pair).wait_recv()
        gxs[kk] = (gs[kk, 2 * c + 1 - xl].astype(F32) + grecv[kk, 1 - xl].astype(F32)).astype(BF16)
        cp = rcopy(gxs.at[kk], gxr.at[kk], g_sem.at[2, kk], g_sem.at[3, kk], xpart)
        cp.start()
        pending.append(cp)

    def back_pair(t):
        yy = (y + t) % NY
        for j in range(2):
            rows = pmat[pl.ds(pl.multiple_of((yy * 2 + j) * 176, 16), 176), :]
            bsend[yy, j] = nn(rows, grad[0:576, :]).astype(BF16)
        if t:
            o = (3 - t) % NY
            cp = rcopy(bsend.at[yy], byr.at[o], b_sem.at[0, t], b_sem.at[1, o], at_mp(yy * 2 + xh))
            cp.start()
            pending.append(cp)

    for t in (2, 1, 3, 0):
        back_pair(t)

    gz_pending = []
    for kk in order:
        rcopy(gxr.at[kk], gxr.at[kk], g_sem.at[2, kk], g_sem.at[3, kk], xpart).wait_recv()
        v = gs[kk, 2 * c + xl].astype(F32) + grecv[kk, xl].astype(F32) + gxr[kk].astype(F32)
        gzs[kk] = v.astype(BF16)
        if kk is not z:
            cp = rcopy(gzs.at[kk], gzr.at[z], g_sem.at[4, kk], g_sem.at[5, z], at_z(kk))
            cp.start()
            pending.append(cp)

    for o in range(1, NZ):
        zz = (z + o) % NZ
        rcopy(lossz.at[zz], lossz.at[zz], l_sem.at[0, o], l_sem.at[1, zz], at_z(zz)).wait_recv()
    loss = lossz[0]
    for zz in range(1, NZ):
        loss = loss + lossz[zz]
    lossx[0] = loss
    cp = rcopy(lossx.at[0], lossx.at[1], l_sem.at[2, 0], l_sem.at[2, 1], xpart)
    cp.start()
    pending.append(cp)

    for o in range(3):
        rcopy(byr.at[o], byr.at[o], b_sem.at[0, 0], b_sem.at[1, o], xhpart).wait_recv()

    def back_sum(j):
        v = bsend[y, j].astype(F32)
        for o in range(3):
            v = v + byr[o, j].astype(F32)
        return v

    bxs[...] = back_sum(1 - xh).astype(BF16)
    bcp = rcopy(bxs, bxr, b_sem.at[2, 0], b_sem.at[2, 1], xhpart)
    bcp.start()
    pending.append(bcp)

    total = gzs[z].astype(F32)
    for o in range(1, NZ):
        zz = (z + o) % NZ
        rcopy(gzr.at[zz], gzr.at[zz], g_sem.at[4, zz], g_sem.at[5, zz], at_z(zz)).wait_recv()
        total = total + gzr[zz].astype(F32)
    q_own = 2 * c + xl
    q_x = 2 * c + 1 - xl
    ag[z, q_own] = (total * (head_scale / token_total)).astype(BF16)

    def ag_send(ref, ssem, rsem, device):
        cp = rcopy(ref, ref, ssem, rsem, device)
        cp.start()
        pending.append(cp)

    mine = ag.at[z, q_own]
    for o in Z_ORDER:
        zz = (z + o) % NZ
        ag_send(mine, agz_sem.at[0, zz], agz_sem.at[1, z], at_z(zz))
    ag_send(mine, agx_sem.at[0, z], agx_sem.at[1, z], xpart)
    ag_send(mine, agp_sem.at[0, z, xl], agp_sem.at[1, z, xl], pair)

    rcopy(lossx.at[0], lossx.at[1], l_sem.at[2, 0], l_sem.at[2, 1], xpart).wait_recv()
    lossc[0] = lossx[0] + lossx[1]
    cp = rcopy(lossc.at[0], lossc.at[1], l_sem.at[3, 0], l_sem.at[3, 1], pair)
    cp.start()
    pending.append(cp)
    bcp.wait_recv()
    bfin[...] = back_sum(xh) + bxr[...].astype(F32)
    back_store = pltpu.make_async_copy(bfin, back_out, out_sem.at[8])
    back_store.start()

    zs = [z] + [(z + o) % NZ for o in (1, 7, 2, 6, 3, 5, 4)]
    for zz in zs:
        if zz is not z:
            ref = ag.at[zz, q_own]
            rcopy(ref, ref, agz_sem.at[0, zz], agz_sem.at[1, zz], at_z(zz)).wait_recv()
            ag_send(ref, agx_sem.at[0, zz], agx_sem.at[1, zz], xpart)
            ag_send(ref, agp_sem.at[0, zz, xl], agp_sem.at[1, zz, xl], pair)
    for zz in zs:
        ref = ag.at[zz, q_x]
        rcopy(ref, ref, agx_sem.at[0, zz], agx_sem.at[1, zz], xpart).wait_recv()
        ag_send(ref, agp_sem.at[0, zz, 1 - xl], agp_sem.at[1, zz, 1 - xl], pair)

    rcopy(lossc.at[0], lossc.at[1], l_sem.at[3, 0], l_sem.at[3, 1], pair).wait_recv()
    lossv[...] = (lossc[0] + lossc[1]) / token_total
    loss_store = pltpu.make_async_copy(lossv, loss_out, out_sem.at[9])
    loss_store.start()

    stores = [back_store, loss_store]
    for zz in range(NZ):
        for x in range(2):
            ref = ag.at[zz, 2 * (1 - c) + x]
            rcopy(ref, ref, agp_sem.at[0, zz, x], agp_sem.at[1, zz, x], pair).wait_recv()
        n = 80 if zz < 7 else 16
        for q in range(4):
            w = 384 if q < 3 else 256
            fout[80 * zz : 80 * zz + n, 384 * q : 384 * q + w] = ag[zz, q, 0:n, 0:w].astype(F32)
        src = fout.at[pl.ds(80 * zz, n)]
        dst = gp6_out.at[pl.ds(80 * zz, n)] if zz < 5 else gpg_out.at[pl.ds(80 * zz - 400, n)]
        cp = pltpu.make_async_copy(src, dst, out_sem.at[zz])
        cp.start()
        stores.append(cp)

    for away, descriptor in ysends:

        @pl.when(away)
        def _(descriptor=descriptor):
            descriptor().wait_send()

    for cp in pending:
        cp.wait_send()
    for cp in stores:
        cp.wait()


def local(
    student_feats,
    keep_index,
    hidden_six,
    resid_six,
    down_six,
    hidden_giant,
    resid_giant,
    down_giant,
    proj_six,
    proj_giant,
):
    token_total = 336 * 32
    dma = pltpu.SemaphoreType.DMA
    hbm = pl.BlockSpec(memory_space=pl.ANY)
    vmem = pl.BlockSpec(memory_space=pltpu.VMEM)
    scratch = [
        pltpu.VMEM((100, 1600), BF16),
        pltpu.VMEM((44, 768), BF16),
        pltpu.VMEM((32, 112, 1664), BF16),
        pltpu.VMEM((32, 48, 768), BF16),
        pltpu.VMEM((3, 560, 1600), BF16),
        pltpu.VMEM((3, 560, 768), BF16),
        pltpu.VMEM((3, 400, 560), BF16),
        pltpu.VMEM((3, 176, 560), BF16),
        pltpu.VMEM((336, 1664), BF16),
        pltpu.VMEM((336, 768), BF16),
        pltpu.VMEM((336, 1408), BF16),
        pltpu.VMEM((576, 1408), BF16),
        pltpu.VMEM((1408, 576), BF16),
        pltpu.VMEM((32, 160, 336), BF16),
        pltpu.VMEM((3, 4, 2, 160, 336), BF16),
        pltpu.VMEM((2, 2, 160, 336), BF16),
        pltpu.VMEM((2, 2, 160, 336), BF16),
        pltpu.VMEM((576, 336), F32),
        pltpu.VMEM((576, 336), F32),
        pltpu.VMEM((8, 8, 336), F32),
        pltpu.VMEM((640, 336), BF16),
        pltpu.VMEM((NZ, 4, 80, 384), BF16),
        pltpu.VMEM((NZ, 2, 80, 384), BF16),
        pltpu.VMEM((NZ, 80, 384), BF16),
        pltpu.VMEM((NZ, 80, 384), BF16),
        pltpu.VMEM((NZ, 80, 384), BF16),
        pltpu.VMEM((NZ, 80, 384), BF16),
        pltpu.VMEM((NZ, 4, 80, 384), BF16),
        pltpu.VMEM((576, 1408), F32),
        pltpu.VMEM((NY, 2, 176, 336), BF16),
        pltpu.VMEM((3, 2, 176, 336), BF16),
        pltpu.VMEM((176, 336), BF16),
        pltpu.VMEM((176, 336), BF16),
        pltpu.VMEM((176, 336), F32),
        pltpu.VMEM((NZ, 8, 128), F32),
        pltpu.VMEM((2, 8, 128), F32),
        pltpu.VMEM((2, 8, 128), F32),
        pltpu.VMEM((8, 128), F32),
        dma((9,)),
        dma((3, 15)),
        dma((3, 15)),
        dma((3, 16)),
        dma((3, 16)),
        dma((16,)),
        dma((3, 4)),
        dma((2, 2)),
        dma((2, 8)),
        dma((6, 8)),
        dma((2, 8)),
        dma((2, 8)),
        dma((2, 8, 2)),
        dma((3, 4)),
        dma((4, 8)),
        dma((10,)),
    ]
    gp6, gpg, back, loss = pl.pallas_call(
        functools.partial(kernel, token_total),
        out_shape=(
            jax.ShapeDtypeStruct((400, 1408), F32),
            jax.ShapeDtypeStruct((176, 1408), F32),
            jax.ShapeDtypeStruct((176, 336), F32),
            jax.ShapeDtypeStruct((8, 128), F32),
        ),
        in_specs=[vmem, vmem] + [hbm] * 9,
        out_specs=(hbm, hbm, hbm, hbm),
        scratch_shapes=scratch,
        compiler_params=pltpu.CompilerParams(
            collective_id=0, has_side_effects=True, vmem_limit_bytes=62 * 1024 * 1024
        ),
        cost_estimate=pl.CostEstimate(flops=6_000_000_000, bytes_accessed=20_000_000, transcendentals=0),
    )(
        keep_index.reshape(1, 336),
        keep_index.reshape(336, 1),
        student_feats.reshape(336, 1408),
        hidden_six,
        resid_six.transpose(0, 2, 1),
        down_six.T,
        hidden_giant,
        resid_giant.transpose(0, 2, 1),
        down_giant.T,
        proj_six.T,
        proj_giant.T,
    )
    grad_student = back.reshape(176, 3, 112).transpose(1, 2, 0)
    return (grad_student, gp6.T, gpg.T, loss[0, 0])


def solution(mesh):
    return jax.shard_map(
        local,
        mesh=mesh,
        in_specs=(
            P("dp", None, None),
            P("dp", None),
            P("dp", None, "mp"),
            P("dp", None, "mp"),
            P("mp", "dp"),
            P("dp", None, "mp"),
            P("dp", None, "mp"),
            P("mp", "dp"),
            P(None, "mp"),
            P(None, "mp"),
        ),
        out_specs=(P("dp", None, "mp"), P(None, "mp"), P(None, "mp"), P()),
        check_vma=False,
    )
```

```python
import functools

import jax
import jax.numpy as jnp
from jax import lax
from jax.experimental import pallas as pl
from jax.experimental.pallas import tpu as pltpu
from jax.sharding import PartitionSpec as P

loss_scale = 256.0
head_scale = 64.0
norm_eps = 1e-06

NZ = 8
NY = 4
F32 = jnp.float32
BF16 = jnp.bfloat16
MESH = pl.DeviceIdType.MESH

SENDS = (
    ((0, 0), (0, 0), (0, 0)),
    ((0, -1), (0, 1), (0, -1)),
    ((0, -2), (0, 2), (0, -2)),
    ((0, -3), (1, 0), (0, 3)),
    ((1, -2), (1, 1), (0, 4)),
)
RECVS = (
    ((0, -1), (0, 1), (1, 0)),
    ((0, -2), (0, 2), (1, -1)),
    ((0, -3), (0, 3), (1, -2)),
    ((0, -4), (1, 1), (1, 3)),
    ((1, -3), (1, 2), (1, 4)),
)
STEPS = len(SENDS)
OWN = 3 * STEPS
Z_ORDER = (4, 3, 5, 2, 6, 1, 7)


def nt(a, b):
    return lax.dot_general(a, b, (((1,), (1,)), ((), ())), preferred_element_type=F32)


def nn(a, b):
    return lax.dot_general(a, b, (((1,), (0,)), ((), ())), preferred_element_type=F32)


def kernel(
    token_total,
    keep,
    stu_hbm,
    h6_hbm,
    r6_hbm,
    w6_hbm,
    hg_hbm,
    rg_hbm,
    wg_hbm,
    p6_hbm,
    pg_hbm,
    gp6_out,
    gpg_out,
    back_out,
    loss_out,
    w6_in,
    wg_in,
    gath6,
    gathg,
    h6,
    hg,
    r6,
    rg,
    rows6,
    rowsg,
    stu,
    pt,
    pmat,
    part,
    yrecv,
    xsend,
    xrecv,
    wpad,
    yrel,
    tgt,
    outs,
    stats,
    grad,
    gs,
    grecv,
    gxs,
    gxr,
    gzs,
    gzr,
    ag,
    bsend,
    byr,
    bxs,
    bxr,
    bfin,
    lossz,
    lossx,
    lossc,
    load_sem,
    wsend_sem,
    wrecv_sem,
    psend_sem,
    precv_sem,
    ysend_sem,
    yrecv_sem,
    yrel_sem,
    xh_sem,
    st_sem,
    g_sem,
    agz_sem,
    agx_sem,
    agp_sem,
    b_sem,
    l_sem,
    out_sem,
):
    dp = lax.axis_index("dp")
    mp = lax.axis_index("mp")
    c = dp % 2
    z = (dp // 2) % NZ
    xl = dp // (2 * NZ)
    y = mp // 2
    xh = mp % 2

    pair = {"dp": dp + 1 - 2 * c}
    xpart = {"dp": (1 - xl) * 2 * NZ + z * 2 + c}
    xhpart = {"mp": y * 2 + 1 - xh}

    def at_z(zz):
        return {"dp": xl * 2 * NZ + zz * 2 + c}

    def at_mp(m):
        return {"mp": m}

    zup = at_z((z + 1) % NZ)
    yup = at_mp(((y + 1) % NY) * 2 + xh)
    ydown = at_mp(((y + NY - 1) % NY) * 2 + xh)
    zdown = at_z((z + NZ - 1) % NZ)

    def rcopy(src, dst, ssem, rsem, device):
        return pltpu.make_async_remote_copy(
            src_ref=src, dst_ref=dst, send_sem=ssem, recv_sem=rsem, device_id=device, device_id_type=MESH
        )

    loads = [
        pltpu.make_async_copy(src, dst, load_sem.at[i])
        for i, (src, dst) in enumerate(
            (
                (w6_hbm, w6_in),
                (wg_hbm, wg_in),
                (h6_hbm, h6),
                (hg_hbm, hg),
                (stu_hbm, stu),
                (p6_hbm, pt.at[pl.ds(0, 400)]),
                (pg_hbm, pt.at[pl.ds(400, 176)]),
                (r6_hbm, r6),
                (rg_hbm, rg),
            )
        )
    ]
    for load in loads:
        load.start()

    barrier = pltpu.get_barrier_semaphore()
    peers = [pair, xpart]
    peers += [at_z((z + o) % NZ) for o in range(1, NZ)]
    peers += [at_mp((mp + o) % 8) for o in range(1, 8)]
    for device in peers:
        pl.semaphore_signal(barrier, inc=1, device_id=device, device_id_type=MESH)

    def slot_of(block):
        plane, off = block
        pl_ = xl if plane == 0 else 1 - xl
        return pl_ * 2 * NZ + ((z + off + NZ) % NZ) * 2

    own = dp
    loads[0].wait()
    loads[1].wait()
    gath6[own] = jnp.zeros((112, 1664), BF16)
    gath6[own, 0:100, 0:1600] = w6_in[...]
    wpad[0:4, :] = jnp.zeros((4, 768), F32)
    wpad[4:48, :] = wg_in[...].astype(F32)
    gathg[own] = wpad[...].astype(BF16)

    pl.semaphore_wait(barrier, len(peers))

    def piece(p, slot):
        if p == 0:
            return gath6.at[slot, pl.ds(0, 64)]
        if p == 1:
            return gath6.at[slot, pl.ds(64, 48)]
        return gathg.at[slot]

    wtargets = (zup, zdown, xpart)
    pending = []

    def send_w(s, k, p):
        ref = piece(p, slot_of(SENDS[s][k]) + c)
        cp = rcopy(ref, ref, wsend_sem.at[p, 3 * s + k], wrecv_sem.at[p, 3 * s + k], wtargets[k])
        cp.start()
        pending.append(cp)

    def send_pair(unit, block, p):
        ref = piece(p, slot_of(block) + c)
        cp = rcopy(ref, ref, psend_sem.at[p, unit], precv_sem.at[p, unit], pair)
        cp.start()
        pending.append(cp)

    def wait_w(s, k, p):
        ref = piece(p, slot_of(RECVS[s][k]) + c)
        rcopy(ref, ref, wsend_sem.at[p, 3 * s + k], wrecv_sem.at[p, 3 * s + k], wtargets[k]).wait_recv()

    for p in range(3):
        for k in range(3):
            send_w(0, k, p)
    for p in range(3):
        send_pair(OWN, (0, 0), p)

    def column(row):
        a = lax.broadcasted_iota(jnp.int32, (112, 112), 0)
        b = lax.broadcasted_iota(jnp.int32, (112, 112), 1)
        return jnp.sum(jnp.where(a == b, row.astype(F32), 0.0), axis=1, keepdims=True)

    rows6[:, 1536:1664] = jnp.zeros((336, 128), BF16)
    def pick_rows(i):
        lane = lax.broadcasted_iota(jnp.int32, (112, 560), 1).astype(F32)
        pick = (column(keep[i : i + 1, :]) == lane).astype(F32).astype(BF16)
        rows6[112 * i : 112 * i + 112, 0:1600] = nn(pick, h6[i]).astype(BF16)
        rowsg[112 * i : 112 * i + 112, :] = nn(pick, hg[i]).astype(BF16)

    loads[2].wait()
    loads[3].wait()
    pick_rows(0)
    pick_rows(1)

    ysends = []
    relays = []
    relayed = 0

    def compute(unit, block):
        slot = slot_of(block)
        for p in range(3):
            ref = piece(p, slot + 1 - c)
            rcopy(ref, ref, psend_sem.at[p, unit], precv_sem.at[p, unit], pair).wait_recv()
        six = nt(gath6[pl.ds(slot, 2)].reshape(224, 1664), rows6[...])
        giant = nt(gathg[pl.ds(slot, 2)].reshape(96, 768), rowsg[...])
        for cc in range(2):
            a = six[112 * cc : 112 * cc + 112]
            b = giant[48 * cc : 48 * cc + 48]
            part[slot + cc, 0:96, :] = a[0:96].astype(BF16)
            part[slot + cc, 96:112, :] = (a[96:112] + b[0:16]).astype(BF16)
            part[slot + cc, 112:144, :] = b[16:48].astype(BF16)
        role = (y - slot // 8 + NY) % NY
        u = (slot // 2) % 4

        def send(cond, src, dst, ssem, rsem, device):
            @pl.when(cond)
            def _():
                rcopy(src, dst, ssem, rsem, device).start()

            ysends.append((cond, lambda: rcopy(src, dst, ssem, rsem, device)))

        first, second = part.at[slot], part.at[slot + 1]
        send(role == 2, first, yrel.at[unit], ysend_sem.at[unit, 0], yrel_sem.at[unit], ydown)
        send(role == 2, second, yrel.at[unit], ysend_sem.at[unit, 1], yrel_sem.at[unit], yup)
        send(role == 1, second, yrecv.at[0, u, 1], ysend_sem.at[unit, 0], yrecv_sem.at[0, u, 1], ydown)
        send(role == 3, first, yrecv.at[1, u, 0], ysend_sem.at[unit, 0], yrecv_sem.at[1, u, 0], yup)

        def relay():
            for want, cc, side, device in ((1, 0, 0, ydown), (3, 1, 1, yup)):
                src, dst = part.at[slot + cc], yrecv.at[side, u, cc]
                ssem, rsem = ysend_sem.at[unit, 1], yrecv_sem.at[side, u, cc]

                @pl.when(role == want)
                def _(cc=cc, src=src, dst=dst, ssem=ssem, rsem=rsem, device=device):
                    ref = yrel.at[unit]
                    rcopy(ref, ref, ssem, yrel_sem.at[unit], device).wait_recv()
                    part[slot + cc] = (part[slot + cc].astype(F32) + yrel[unit].astype(F32)).astype(BF16)
                    rcopy(src, dst, ssem, rsem, device).start()

                ysends.append((role == want, lambda src=src, dst=dst, ssem=ssem, rsem=rsem, device=device: rcopy(src, dst, ssem, rsem, device)))

        relays.append(relay)

    def head_out(i):
        if i == 0:
            for load in loads[4:]:
                load.wait()
        outs[192 * i : 192 * i + 192, :] = nt(pt[192 * i : 192 * i + 192, :], stu[...])

    def turn_heads(lo, hi):
        for l in range(lo, hi):
            pmat[128 * l : 128 * l + 128, :] = pt[:, 128 * l : 128 * l + 128].T

    def residuals(i):
        row = jnp.concatenate([keep[j : j + 1, :] for j in range(3)], axis=1)
        pos = lax.broadcasted_iota(jnp.int32, (560, 336), 0)
        col = lax.broadcasted_iota(jnp.int32, (560, 336), 1)
        clip = (col >= 112 * i) & (col < 112 * i + 112)
        pick = ((row == pos) & clip).astype(F32).astype(BF16)
        a = nn(r6[i], pick)
        b = nn(rg[i], pick)
        if i == 0:
            tgt[0:400, :] = a
            tgt[400:576, :] = b
        else:
            tgt[0:400, :] += a
            tgt[400:576, :] += b

    work = [functools.partial(head_out, i) for i in range(3)]
    work += [functools.partial(residuals, i) for i in range(3)]
    work += [functools.partial(turn_heads, 0, 6), functools.partial(turn_heads, 6, 11)]

    for s in range(STEPS):
        for p in range(3):
            for k in range(3):
                wait_w(s, k, p)
            if s + 1 < STEPS:
                for k in range(3):
                    send_w(s + 1, k, p)
            for k in range(3):
                send_pair(3 * s + k, RECVS[s][k], p)
            if s > 0:
                compute(3 * (s - 1) + p, RECVS[s - 1][p])
            elif p == 0:
                pick_rows(2)
            elif p == 1:
                compute(OWN, (0, 0))
            if p != (1 if s == 0 else 2) and s + p > 0 and work:
                work.pop(0)()
            while len(relays) - relayed > 2:
                relays[relayed]()
                relayed += 1
    while work:
        work.pop(0)()

    def summed(u, cc):
        total = part[y * 8 + u * 2 + cc].astype(F32)
        for side in range(2):
            total = total + yrecv[side, u, cc].astype(F32)
        return total

    def wait_y(u):
        for side in range(2):
            for cc in range(2):
                ref = yrecv.at[side, u, cc]
                rcopy(ref, ref, ysend_sem.at[0, 0], yrecv_sem.at[side, u, cc], xhpart).wait_recv()

    def xh_copy(k):
        return rcopy(xsend.at[k], xrecv.at[k], xh_sem.at[0, k], xh_sem.at[1, k], xhpart)

    def exchange():
        for k in range(2):
            u = 2 * (1 - xh) + k
            wait_y(u)
            for cc in range(2):
                xsend[k, cc] = summed(u, cc).astype(BF16)
            xh_copy(k).start()

    def targets():
        for k in range(2):
            u = 2 * xh + k
            wait_y(u)
            xh_copy(k).wait_recv()
            for cc in range(2):
                total = summed(u, cc) + xrecv[k, cc].astype(F32)
                f = 100 * (2 * k + cc)
                tgt[f : f + 100, :] += total[0:100]
                f = 400 + 44 * (2 * k + cc)
                tgt[f : f + 44, :] += total[100:144]

    early = y // 2 == xl
    for i in range(relayed, len(relays)):
        relays[i]()
    relayed = len(relays)
    pl.when(early)(exchange)
    for k in range(3):
        compute(3 * (STEPS - 1) + k, RECVS[STEPS - 1][k])
    for i in range(relayed, len(relays)):
        relays[i]()
    pl.when(jnp.logical_not(early))(exchange)
    targets()

    def sums(lo, hi):
        t = tgt[lo:hi, :]
        o = outs[lo:hi, :]
        return [
            jnp.sum(o * t, axis=0, keepdims=True),
            jnp.sum(o * o, axis=0, keepdims=True),
            jnp.sum(t * t, axis=0, keepdims=True),
        ]

    for i, row in enumerate(sums(0, 400) + sums(400, 576)):
        stats[mp, i : i + 1, :] = row
    for i in range(6, 8):
        stats[mp, i : i + 1, :] = jnp.zeros((1, 336), F32)
    st = []
    for o in range(1, 8):
        m = (mp + o) % 8
        cp = rcopy(stats.at[mp], stats.at[mp], st_sem.at[0, o], st_sem.at[1, mp], at_mp(m))
        cp.start()
        pending.append(cp)
    for o in range(1, 8):
        m = (mp + o) % 8
        rcopy(stats.at[m], stats.at[m], st_sem.at[0, o], st_sem.at[1, m], at_mp(m)).wait_recv()
    total = stats[0]
    for m in range(1, 8):
        total = total + stats[m]

    def gradient(lo, hi, i):
        norm_out = jnp.sqrt(total[i + 1 : i + 2] + norm_eps)
        norm_tar = jnp.sqrt(total[i + 2 : i + 3] + norm_eps)
        both = norm_out * norm_tar
        cosine = total[i : i + 1] / both
        a = -loss_scale / both
        b = loss_scale * cosine / (norm_out * norm_out)
        grad[lo:hi, :] = (tgt[lo:hi, :] * a + outs[lo:hi, :] * b).astype(BF16)
        return cosine

    cos6 = gradient(0, 400, 0)
    cosg = gradient(400, 576, 3)
    grad[576:640, :] = jnp.zeros((64, 336), BF16)
    loss_local = jnp.sum(2.0 - cos6 - cosg, axis=1, keepdims=True)
    lossz[z] = jnp.broadcast_to(loss_local, (8, 128))
    for o in range(1, NZ):
        zz = (z + o) % NZ
        cp = rcopy(lossz.at[z], lossz.at[z], l_sem.at[0, o], l_sem.at[1, z], at_z(zz))
        cp.start()
        pending.append(cp)

    order = [(z + o) % NZ for o in Z_ORDER] + [z]
    for kk in order:
        rows = grad[pl.ds(pl.multiple_of(kk * 80, 16), 80), :]
        g = nn(rows, stu[...]).astype(BF16)
        for q in range(3):
            gs[kk, q] = g[:, 384 * q : 384 * q + 384]
        gs[kk, 3, :, 0:256] = g[:, 1152:1408]
        gs[kk, 3, :, 256:384] = jnp.zeros((80, 128), BF16)
        cp = rcopy(gs.at[kk, pl.ds(2 * (1 - c), 2)], grecv.at[kk], g_sem.at[0, kk], g_sem.at[1, kk], pair)
        cp.start()
        pending.append(cp)

    for kk in order:
        rcopy(grecv.at[kk], grecv.at[kk], g_sem.at[0, kk], g_sem.at[1, kk], pair).wait_recv()
        gxs[kk] = (gs[kk, 2 * c + 1 - xl].astype(F32) + grecv[kk, 1 - xl].astype(F32)).astype(BF16)
        cp = rcopy(gxs.at[kk], gxr.at[kk], g_sem.at[2, kk], g_sem.at[3, kk], xpart)
        cp.start()
        pending.append(cp)

    def back_pair(t):
        yy = (y + t) % NY
        for j in range(2):
            rows = pmat[pl.ds(pl.multiple_of((yy * 2 + j) * 176, 16), 176), :]
            bsend[yy, j] = nn(rows, grad[0:576, :]).astype(BF16)
        if t:
            o = (3 - t) % NY
            cp = rcopy(bsend.at[yy], byr.at[o], b_sem.at[0, t], b_sem.at[1, o], at_mp(yy * 2 + xh))
            cp.start()
            pending.append(cp)

    for t in (2, 1, 3, 0):
        back_pair(t)

    gz_pending = []
    for kk in order:
        rcopy(gxr.at[kk], gxr.at[kk], g_sem.at[2, kk], g_sem.at[3, kk], xpart).wait_recv()
        v = gs[kk, 2 * c + xl].astype(F32) + grecv[kk, xl].astype(F32) + gxr[kk].astype(F32)
        gzs[kk] = v.astype(BF16)
        if kk is not z:
            cp = rcopy(gzs.at[kk], gzr.at[z], g_sem.at[4, kk], g_sem.at[5, z], at_z(kk))
            cp.start()
            pending.append(cp)

    for o in range(1, NZ):
        zz = (z + o) % NZ
        rcopy(lossz.at[zz], lossz.at[zz], l_sem.at[0, o], l_sem.at[1, zz], at_z(zz)).wait_recv()
    loss = lossz[0]
    for zz in range(1, NZ):
        loss = loss + lossz[zz]
    lossx[0] = loss
    cp = rcopy(lossx.at[0], lossx.at[1], l_sem.at[2, 0], l_sem.at[2, 1], xpart)
    cp.start()
    pending.append(cp)

    for o in range(3):
        rcopy(byr.at[o], byr.at[o], b_sem.at[0, 0], b_sem.at[1, o], xhpart).wait_recv()

    def back_sum(j):
        v = bsend[y, j].astype(F32)
        for o in range(3):
            v = v + byr[o, j].astype(F32)
        return v

    bxs[...] = back_sum(1 - xh).astype(BF16)
    bcp = rcopy(bxs, bxr, b_sem.at[2, 0], b_sem.at[2, 1], xhpart)
    bcp.start()
    pending.append(bcp)

    total = gzs[z].astype(F32)
    for o in range(1, NZ):
        zz = (z + o) % NZ
        rcopy(gzr.at[zz], gzr.at[zz], g_sem.at[4, zz], g_sem.at[5, zz], at_z(zz)).wait_recv()
        total = total + gzr[zz].astype(F32)
    q_own = 2 * c + xl
    q_x = 2 * c + 1 - xl
    ag[z, q_own] = (total * (head_scale / token_total)).astype(BF16)

    def ag_send(ref, ssem, rsem, device):
        cp = rcopy(ref, ref, ssem, rsem, device)
        cp.start()
        pending.append(cp)

    mine = ag.at[z, q_own]
    for o in Z_ORDER:
        zz = (z + o) % NZ
        ag_send(mine, agz_sem.at[0, zz], agz_sem.at[1, z], at_z(zz))
    ag_send(mine, agx_sem.at[0, z], agx_sem.at[1, z], xpart)
    ag_send(mine, agp_sem.at[0, z, xl], agp_sem.at[1, z, xl], pair)

    rcopy(lossx.at[0], lossx.at[1], l_sem.at[2, 0], l_sem.at[2, 1], xpart).wait_recv()
    lossc[0] = lossx[0] + lossx[1]
    cp = rcopy(lossc.at[0], lossc.at[1], l_sem.at[3, 0], l_sem.at[3, 1], pair)
    cp.start()
    pending.append(cp)
    bcp.wait_recv()
    v = back_sum(xh) + bxr[...].astype(F32)
    for i in range(3):
        bfin[i] = v[:, 112 * i : 112 * i + 112]
    back_store = pltpu.make_async_copy(bfin, back_out, out_sem.at[8, 0])
    back_store.start()

    zs = [z] + [(z + o) % NZ for o in (1, 7, 2, 6, 3, 5, 4)]
    for zz in zs:
        if zz is not z:
            ref = ag.at[zz, q_own]
            rcopy(ref, ref, agz_sem.at[0, zz], agz_sem.at[1, zz], at_z(zz)).wait_recv()
            ag_send(ref, agx_sem.at[0, zz], agx_sem.at[1, zz], xpart)
            ag_send(ref, agp_sem.at[0, zz, xl], agp_sem.at[1, zz, xl], pair)
    for zz in zs:
        ref = ag.at[zz, q_x]
        rcopy(ref, ref, agx_sem.at[0, zz], agx_sem.at[1, zz], xpart).wait_recv()
        ag_send(ref, agp_sem.at[0, zz, 1 - xl], agp_sem.at[1, zz, 1 - xl], pair)

    rcopy(lossc.at[0], lossc.at[1], l_sem.at[3, 0], l_sem.at[3, 1], pair).wait_recv()
    loss_out[...] = (lossc[0, 0:1, 0:1] + lossc[1, 0:1, 0:1]) / token_total

    stores = [back_store]
    for zz in range(NZ):
        for x in range(2):
            ref = ag.at[zz, 2 * (1 - c) + x]
            rcopy(ref, ref, agp_sem.at[0, zz, x], agp_sem.at[1, zz, x], pair).wait_recv()
        n = 80 if zz < 7 else 16
        out, lo = (gp6_out, 80 * zz) if zz < 5 else (gpg_out, 80 * zz - 400)
        for q in range(4):
            w = 384 if q < 3 else 256
            cp = pltpu.make_async_copy(
                ag.at[zz, q, pl.ds(0, n), pl.ds(0, w)], out.at[pl.ds(lo, n), pl.ds(384 * q, w)], out_sem.at[zz, q]
            )
            cp.start()
            stores.append(cp)

    for away, descriptor in ysends:

        @pl.when(away)
        def _(descriptor=descriptor):
            descriptor().wait_send()

    for k in range(2):
        xh_copy(k).wait_send()
    for cp in pending:
        cp.wait_send()
    for cp in stores:
        cp.wait()


def local(
    student_feats,
    keep_index,
    hidden_six,
    resid_six,
    down_six,
    hidden_giant,
    resid_giant,
    down_giant,
    proj_six,
    proj_giant,
):
    token_total = 336 * 32
    dma = pltpu.SemaphoreType.DMA
    hbm = pl.BlockSpec(memory_space=pl.ANY)
    vmem = pl.BlockSpec(memory_space=pltpu.VMEM)
    scratch = [
        pltpu.VMEM((100, 1600), BF16),
        pltpu.VMEM((44, 768), BF16),
        pltpu.VMEM((32, 112, 1664), BF16),
        pltpu.VMEM((32, 48, 768), BF16),
        pltpu.VMEM((3, 560, 1600), BF16),
        pltpu.VMEM((3, 560, 768), BF16),
        pltpu.VMEM((3, 400, 560), BF16),
        pltpu.VMEM((3, 176, 560), BF16),
        pltpu.VMEM((336, 1664), BF16),
        pltpu.VMEM((336, 768), BF16),
        pltpu.VMEM((336, 1408), BF16),
        pltpu.VMEM((576, 1408), BF16),
        pltpu.VMEM((1408, 576), BF16),
        pltpu.VMEM((32, 144, 336), BF16),
        pltpu.VMEM((2, 4, 2, 144, 336), BF16),
        pltpu.VMEM((2, 2, 144, 336), BF16),
        pltpu.VMEM((2, 2, 144, 336), BF16),
        pltpu.VMEM((48, 768), F32),
        pltpu.VMEM((16, 144, 336), BF16),
        pltpu.VMEM((576, 336), F32),
        pltpu.VMEM((576, 336), F32),
        pltpu.VMEM((8, 8, 336), F32),
        pltpu.VMEM((640, 336), BF16),
        pltpu.VMEM((NZ, 4, 80, 384), BF16),
        pltpu.VMEM((NZ, 2, 80, 384), BF16),
        pltpu.VMEM((NZ, 80, 384), BF16),
        pltpu.VMEM((NZ, 80, 384), BF16),
        pltpu.VMEM((NZ, 80, 384), BF16),
        pltpu.VMEM((NZ, 80, 384), BF16),
        pltpu.VMEM((NZ, 4, 80, 384), BF16),
        pltpu.VMEM((NY, 2, 176, 336), BF16),
        pltpu.VMEM((3, 2, 176, 336), BF16),
        pltpu.VMEM((176, 336), BF16),
        pltpu.VMEM((176, 336), BF16),
        pltpu.VMEM((3, 176, 112), F32),
        pltpu.VMEM((NZ, 8, 128), F32),
        pltpu.VMEM((2, 8, 128), F32),
        pltpu.VMEM((2, 8, 128), F32),
        dma((9,)),
        dma((3, 15)),
        dma((3, 15)),
        dma((3, 16)),
        dma((3, 16)),
        dma((16, 2)),
        dma((2, 4, 2)),
        dma((16,)),
        dma((2, 2)),
        dma((2, 8)),
        dma((6, 8)),
        dma((2, 8)),
        dma((2, 8)),
        dma((2, 8, 2)),
        dma((3, 4)),
        dma((4, 8)),
        dma((9, 4)),
    ]
    gp6, gpg, back, loss = pl.pallas_call(
        functools.partial(kernel, token_total),
        out_shape=(
            jax.ShapeDtypeStruct((400, 1408), BF16),
            jax.ShapeDtypeStruct((176, 1408), BF16),
            jax.ShapeDtypeStruct((3, 176, 112), F32),
            jax.ShapeDtypeStruct((1, 1), F32),
        ),
        in_specs=[vmem] + [hbm] * 9,
        out_specs=(hbm, hbm, hbm, vmem),
        scratch_shapes=scratch,
        compiler_params=pltpu.CompilerParams(
            collective_id=0, has_side_effects=True, vmem_limit_bytes=62 * 1024 * 1024
        ),
        cost_estimate=pl.CostEstimate(flops=6_000_000_000, bytes_accessed=20_000_000, transcendentals=0),
    )(
        keep_index,
        student_feats.reshape(336, 1408),
        hidden_six,
        resid_six.transpose(0, 2, 1),
        down_six.T,
        hidden_giant,
        resid_giant.transpose(0, 2, 1),
        down_giant.T,
        proj_six.T,
        proj_giant.T,
    )
    return (back.transpose(0, 2, 1), gp6.astype(F32).T, gpg.astype(F32).T, loss.reshape(()))


def solution(mesh):
    return jax.shard_map(
        local,
        mesh=mesh,
        in_specs=(
            P("dp", None, None),
            P("dp", None),
            P("dp", None, "mp"),
            P("dp", None, "mp"),
            P("mp", "dp"),
            P("dp", None, "mp"),
            P("dp", None, "mp"),
            P("mp", "dp"),
            P(None, "mp"),
            P(None, "mp"),
        ),
        out_specs=(P("dp", None, "mp"), P(None, "mp"), P(None, "mp"), P()),
        check_vma=False,
    )
```

```python
import functools

import jax
import jax.numpy as jnp
from jax import lax
from jax.experimental import pallas as pl
from jax.experimental.pallas import tpu as pltpu
from jax.sharding import PartitionSpec as P

loss_scale = 256.0
head_scale = 64.0
norm_eps = 1e-06

NZ = 8
NY = 4
F32 = jnp.float32
BF16 = jnp.bfloat16
MESH = pl.DeviceIdType.MESH

SENDS = (
    ((0, 0), (0, 0), (0, 0)),
    ((0, -1), (0, 1), (0, -1)),
    ((0, -2), (0, 2), (0, -2)),
    ((0, -3), (1, 0), (0, 3)),
    ((1, -2), (1, 1), (0, 4)),
)
RECVS = (
    ((0, -1), (0, 1), (1, 0)),
    ((0, -2), (0, 2), (1, -1)),
    ((0, -3), (0, 3), (1, -2)),
    ((0, -4), (1, 1), (1, 3)),
    ((1, -3), (1, 2), (1, 4)),
)
STEPS = len(SENDS)
OWN = 3 * STEPS
Z_ORDER = (4, 3, 5, 2, 6, 1, 7)


def nt(a, b):
    return lax.dot_general(a, b, (((1,), (1,)), ((), ())), preferred_element_type=F32)


def nn(a, b):
    return lax.dot_general(a, b, (((1,), (0,)), ((), ())), preferred_element_type=F32)


def kernel(
    token_total,
    keep,
    stu_hbm,
    h6_hbm,
    r6_hbm,
    w6_hbm,
    hg_hbm,
    rg_hbm,
    wg_hbm,
    p6_hbm,
    pg_hbm,
    gp6_out,
    gpg_out,
    back_out,
    loss_out,
    w6_in,
    wg_in,
    gath6,
    gathg,
    h6,
    hg,
    r6,
    rg,
    rows6,
    rowsg,
    stu,
    pt,
    pmat,
    part,
    yrecv,
    xsend,
    xrecv,
    wpad,
    yrel,
    tgt,
    outs,
    stats,
    grad,
    gs,
    grecv,
    gxs,
    gxr,
    gzs,
    gzr,
    ag,
    fout,
    bsend,
    byr,
    bxs,
    bxr,
    bfin,
    lossz,
    lossx,
    lossc,
    load_sem,
    wsend_sem,
    wrecv_sem,
    psend_sem,
    precv_sem,
    ysend_sem,
    yrecv_sem,
    yrel_sem,
    xh_sem,
    st_sem,
    g_sem,
    agz_sem,
    agx_sem,
    agp_sem,
    b_sem,
    l_sem,
    out_sem,
):
    dp = lax.axis_index("dp")
    mp = lax.axis_index("mp")
    c = dp % 2
    z = (dp // 2) % NZ
    xl = dp // (2 * NZ)
    y = mp // 2
    xh = mp % 2

    pair = {"dp": dp + 1 - 2 * c}
    xpart = {"dp": (1 - xl) * 2 * NZ + z * 2 + c}
    xhpart = {"mp": y * 2 + 1 - xh}

    def at_z(zz):
        return {"dp": xl * 2 * NZ + zz * 2 + c}

    def at_mp(m):
        return {"mp": m}

    zup = at_z((z + 1) % NZ)
    yup = at_mp(((y + 1) % NY) * 2 + xh)
    ydown = at_mp(((y + NY - 1) % NY) * 2 + xh)
    zdown = at_z((z + NZ - 1) % NZ)

    def rcopy(src, dst, ssem, rsem, device):
        return pltpu.make_async_remote_copy(
            src_ref=src, dst_ref=dst, send_sem=ssem, recv_sem=rsem, device_id=device, device_id_type=MESH
        )

    barrier = pltpu.get_barrier_semaphore()
    peers = [pair, xpart]
    peers += [at_z((z + o) % NZ) for o in range(1, NZ)]
    peers += [at_mp((mp + o) % 8) for o in range(1, 8)]
    for device in peers:
        pl.semaphore_signal(barrier, inc=1, device_id=device, device_id_type=MESH)

    loads = [
        pltpu.make_async_copy(src, dst, load_sem.at[i])
        for i, (src, dst) in enumerate(
            (
                (w6_hbm, w6_in),
                (wg_hbm, wg_in),
                (h6_hbm, h6),
                (hg_hbm, hg),
                (stu_hbm, stu),
                (p6_hbm, pt.at[pl.ds(0, 400)]),
                (pg_hbm, pt.at[pl.ds(400, 176)]),
                (r6_hbm, r6),
                (rg_hbm, rg),
            )
        )
    ]
    for load in loads[:2]:
        load.start()

    def slot_of(block):
        plane, off = block
        pl_ = xl if plane == 0 else 1 - xl
        return pl_ * 2 * NZ + ((z + off + NZ) % NZ) * 2

    own = dp
    loads[0].wait()
    loads[1].wait()
    gath6[own] = jnp.zeros((112, 1664), BF16)
    gath6[own, 0:100, 0:1600] = w6_in[...]
    wpad[0:4, :] = jnp.zeros((4, 768), F32)
    wpad[4:48, :] = wg_in[...].astype(F32)
    gathg[own] = wpad[...].astype(BF16)

    pl.semaphore_wait(barrier, len(peers))

    def piece(p, slot):
        if p == 0:
            return gath6.at[slot, pl.ds(0, 80)]
        if p == 1:
            return gath6.at[slot, pl.ds(80, 32)]
        return gathg.at[slot]

    wtargets = (zup, zdown, xpart)
    pending = []

    def send_w(s, k, p):
        ref = piece(p, slot_of(SENDS[s][k]) + c)
        cp = rcopy(ref, ref, wsend_sem.at[p, 3 * s + k], wrecv_sem.at[p, 3 * s + k], wtargets[k])
        cp.start()
        pending.append(cp)

    def send_pair(unit, block, p):
        ref = piece(p, slot_of(block) + c)
        cp = rcopy(ref, ref, psend_sem.at[p, unit], precv_sem.at[p, unit], pair)
        cp.start()
        pending.append(cp)

    def wait_w(s, k, p):
        ref = piece(p, slot_of(RECVS[s][k]) + c)
        rcopy(ref, ref, wsend_sem.at[p, 3 * s + k], wrecv_sem.at[p, 3 * s + k], wtargets[k]).wait_recv()

    for p in range(3):
        for k in range(3):
            send_w(0, k, p)
    for p in range(3):
        send_pair(OWN, (0, 0), p)
    for load in loads[2:]:
        load.start()

    def column(row):
        a = lax.broadcasted_iota(jnp.int32, (112, 112), 0)
        b = lax.broadcasted_iota(jnp.int32, (112, 112), 1)
        return jnp.sum(jnp.where(a == b, row.astype(F32), 0.0), axis=1, keepdims=True)

    rows6[:, 1536:1664] = jnp.zeros((336, 128), BF16)
    def pick_rows(i):
        lane = lax.broadcasted_iota(jnp.int32, (112, 560), 1).astype(F32)
        pick = (column(keep[i : i + 1, :]) == lane).astype(F32).astype(BF16)
        rows6[112 * i : 112 * i + 112, 0:1600] = nn(pick, h6[i]).astype(BF16)
        rowsg[112 * i : 112 * i + 112, :] = nn(pick, hg[i]).astype(BF16)

    loads[2].wait()
    loads[3].wait()
    pick_rows(0)
    pick_rows(1)

    ysends = []
    relays = []

    SUBS = ((0, 80), (80, 64))

    def compute(unit, block, sub):
        slot = slot_of(block)
        lo, n = SUBS[sub]
        for p in ((0,), (1, 2))[sub]:
            ref = piece(p, slot + 1 - c)
            rcopy(ref, ref, psend_sem.at[p, unit], precv_sem.at[p, unit], pair).wait_recv()
        if sub == 0:
            six = nt(gath6[pl.ds(slot, 2), 0:80].reshape(160, 1664), rows6[...])
            part[pl.ds(slot, 2), 0:80, :] = six.astype(BF16).reshape(2, 80, 336)
        else:
            six = nt(gath6[pl.ds(slot, 2), 80:112].reshape(64, 1664), rows6[...])
            giant = nt(gathg[pl.ds(slot, 2)].reshape(96, 768), rowsg[...])
            for cc in range(2):
                a = six[32 * cc : 32 * cc + 32]
                b = giant[48 * cc : 48 * cc + 48]
                part[slot + cc, 80:96, :] = a[0:16].astype(BF16)
                part[slot + cc, 96:112, :] = (a[16:32] + b[0:16]).astype(BF16)
                part[slot + cc, 112:144, :] = b[16:48].astype(BF16)
        role = (y - slot // 8 + NY) % NY
        u = (slot // 2) % 4
        rows = pl.ds(lo, n)

        def send(cond, src, dst, ssem, rsem, device):
            @pl.when(cond)
            def _():
                rcopy(src, dst, ssem, rsem, device).start()

            ysends.append((cond, lambda: rcopy(src, dst, ssem, rsem, device)))

        first, second = part.at[slot, rows], part.at[slot + 1, rows]
        rel, rsem = yrel.at[unit, rows], yrel_sem.at[sub, unit]
        s0, s1 = ysend_sem.at[sub, unit, 0], ysend_sem.at[sub, unit, 1]
        send(role == 2, first, rel, s0, rsem, ydown)
        send(role == 2, second, rel, s1, rsem, yup)
        send(role == 1, second, yrecv.at[0, u, 1, rows], s0, yrecv_sem.at[sub, 0, u, 1], ydown)
        send(role == 3, first, yrecv.at[1, u, 0, rows], s0, yrecv_sem.at[sub, 1, u, 0], yup)

        def relay():
            for want, cc, side, device in ((1, 0, 0, ydown), (3, 1, 1, yup)):

                def descriptor(cc=cc, side=side, device=device):
                    dst = yrecv.at[side, u, cc, rows]
                    return rcopy(part.at[slot + cc, rows], dst, s1, yrecv_sem.at[sub, side, u, cc], device)

                @pl.when(role == want)
                def _(cc=cc, device=device, descriptor=descriptor):
                    rcopy(rel, rel, s1, rsem, device).wait_recv()
                    both = part[slot + cc, lo : lo + n].astype(F32) + yrel[unit, lo : lo + n].astype(F32)
                    part[slot + cc, lo : lo + n] = both.astype(BF16)
                    descriptor().start()

                ysends.append((role == want, descriptor))

        relays.append(relay)

    def head_out(i):
        if i == 0:
            for load in loads[4:]:
                load.wait()
        outs[192 * i : 192 * i + 192, :] = nt(pt[192 * i : 192 * i + 192, :], stu[...])

    def turn_heads(lo, hi):
        for l in range(lo, hi):
            pmat[128 * l : 128 * l + 128, :] = pt[:, 128 * l : 128 * l + 128].T

    def residuals(i):
        row = jnp.concatenate([keep[j : j + 1, :] for j in range(3)], axis=1)
        pos = lax.broadcasted_iota(jnp.int32, (560, 336), 0)
        col = lax.broadcasted_iota(jnp.int32, (560, 336), 1)
        clip = (col >= 112 * i) & (col < 112 * i + 112)
        pick = ((row == pos) & clip).astype(F32).astype(BF16)
        a = nn(r6[i], pick)
        b = nn(rg[i], pick)
        if i == 0:
            tgt[0:400, :] = a
            tgt[400:576, :] = b
        else:
            tgt[0:400, :] += a
            tgt[400:576, :] += b

    work = [functools.partial(head_out, i) for i in range(3)]
    work += [functools.partial(residuals, i) for i in range(3)]
    work += [functools.partial(turn_heads, 0, 6), functools.partial(turn_heads, 6, 11)]

    def run_relays(keep_back):
        while len(relays) > keep_back:
            relays.pop(0)()

    for s in range(STEPS):
        for ps in ((0,), (1, 2)):
            for p in ps:
                for k in range(3):
                    wait_w(s, k, p)
                if s + 1 < STEPS:
                    for k in range(3):
                        send_w(s + 1, k, p)
                for k in range(3):
                    send_pair(3 * s + k, RECVS[s][k], p)
            if ps == (0,):
                if s == 0:
                    pick_rows(2)
                    compute(OWN, (0, 0), 0)
                    compute(OWN, (0, 0), 1)
                else:
                    for k in range(3):
                        compute(3 * (s - 1) + k, RECVS[s - 1][k], 1)
                run_relays(3)
                for k in range(3):
                    compute(3 * s + k, RECVS[s][k], 0)
            elif s + 1 < STEPS:
                work.pop(0)()
                work.pop(0)()
                run_relays(3)

    def summed(u, cc, sub):
        lo, n = SUBS[sub]
        total = part[y * 8 + u * 2 + cc, lo : lo + n].astype(F32)
        for side in range(2):
            total = total + yrecv[side, u, cc, lo : lo + n].astype(F32)
        return total

    def wait_y(u, sub):
        for side in range(2):
            for cc in range(2):
                ref = yrecv.at[side, u, cc, pl.ds(*SUBS[sub])]
                rcopy(ref, ref, ysend_sem.at[0, 0, 0], yrecv_sem.at[sub, side, u, cc], xhpart).wait_recv()

    def xh_copy(k, sub):
        rows = pl.ds(*SUBS[sub])
        src, dst = xsend.at[k, pl.ds(0, 2), rows], xrecv.at[k, pl.ds(0, 2), rows]
        return rcopy(src, dst, xh_sem.at[0, k, sub], xh_sem.at[1, k, sub], xhpart)

    def exchange(sub):
        lo, n = SUBS[sub]
        for k in range(2):
            u = 2 * (1 - xh) + k
            wait_y(u, sub)
            for cc in range(2):
                xsend[k, cc, lo : lo + n] = summed(u, cc, sub).astype(BF16)
            xh_copy(k, sub).start()

    def targets(sub):
        for k in range(2):
            u = 2 * xh + k
            wait_y(u, sub)
            xh_copy(k, sub).wait_recv()
            lo, n = SUBS[sub]
            for cc in range(2):
                total = summed(u, cc, sub) + xrecv[k, cc, lo : lo + n].astype(F32)
                f = 100 * (2 * k + cc)
                if sub == 0:
                    tgt[f : f + 80, :] += total
                else:
                    tgt[f + 80 : f + 100, :] += total[0:20]
                    f = 400 + 44 * (2 * k + cc)
                    tgt[f : f + 44, :] += total[20:64]

    early = y // 2 == xl

    @pl.when(early)
    def _():
        exchange(0)
        exchange(1)

    for k in range(3):
        compute(3 * (STEPS - 1) + k, RECVS[STEPS - 1][k], 1)
    run_relays(3)
    pl.when(jnp.logical_not(early))(functools.partial(exchange, 0))
    run_relays(0)
    pl.when(jnp.logical_not(early))(functools.partial(exchange, 1))
    targets(0)
    targets(1)

    def sums(lo, hi):
        t = tgt[lo:hi, :]
        o = outs[lo:hi, :]
        return [
            jnp.sum(o * t, axis=0, keepdims=True),
            jnp.sum(o * o, axis=0, keepdims=True),
            jnp.sum(t * t, axis=0, keepdims=True),
        ]

    for i, row in enumerate(sums(0, 400) + sums(400, 576)):
        stats[mp, i : i + 1, :] = row
    for i in range(6, 8):
        stats[mp, i : i + 1, :] = jnp.zeros((1, 336), F32)
    st = []
    for o in range(1, 8):
        m = (mp + o) % 8
        cp = rcopy(stats.at[mp], stats.at[mp], st_sem.at[0, o], st_sem.at[1, mp], at_mp(m))
        cp.start()
        pending.append(cp)
    for o in range(1, 8):
        m = (mp + o) % 8
        rcopy(stats.at[m], stats.at[m], st_sem.at[0, o], st_sem.at[1, m], at_mp(m)).wait_recv()
    total = stats[0]
    for m in range(1, 8):
        total = total + stats[m]

    def gradient(lo, hi, i):
        norm_out = jnp.sqrt(total[i + 1 : i + 2] + norm_eps)
        norm_tar = jnp.sqrt(total[i + 2 : i + 3] + norm_eps)
        both = norm_out * norm_tar
        cosine = total[i : i + 1] / both
        a = -loss_scale / both
        b = loss_scale * cosine / (norm_out * norm_out)
        grad[lo:hi, :] = (tgt[lo:hi, :] * a + outs[lo:hi, :] * b).astype(BF16)
        return cosine

    cos6 = gradient(0, 400, 0)
    cosg = gradient(400, 576, 3)
    loss_local = jnp.sum(2.0 - cos6 - cosg, axis=1, keepdims=True)
    lossz[z] = jnp.broadcast_to(loss_local, (8, 128))
    for o in range(1, NZ):
        zz = (z + o) % NZ
        cp = rcopy(lossz.at[z], lossz.at[z], l_sem.at[0, o], l_sem.at[1, z], at_z(zz))
        cp.start()
        pending.append(cp)

    order = [(z + o) % NZ for o in Z_ORDER] + [z]

    def head_rows(core):
        rows = grad[pl.ds(pl.multiple_of(core * 288, 16), 288), :]
        g = nn(rows, stu[...]).astype(BF16)
        for x in range(2):
            for r in range(9):
                for l in range(11):
                    t = r * 11 + l
                    lo = 144 * x + 16 * r
                    gs[t // 13, 2 * core + x, t % 13] = g[lo : lo + 16, 128 * l : 128 * l + 128]
            for j in range(8, 13):
                gs[7, 2 * core + x, j] = jnp.zeros((16, 128), BF16)

    head_rows(1 - c)
    for kk in order:
        cp = rcopy(gs.at[kk, pl.ds(2 * (1 - c), 2)], grecv.at[kk], g_sem.at[0, kk], g_sem.at[1, kk], pair)
        cp.start()
        pending.append(cp)
    head_rows(c)

    for kk in order:
        rcopy(grecv.at[kk], grecv.at[kk], g_sem.at[0, kk], g_sem.at[1, kk], pair).wait_recv()
        gxs[kk] = (gs[kk, 2 * c + 1 - xl].astype(F32) + grecv[kk, 1 - xl].astype(F32)).astype(BF16)
        cp = rcopy(gxs.at[kk], gxr.at[kk], g_sem.at[2, kk], g_sem.at[3, kk], xpart)
        cp.start()
        pending.append(cp)

    def back_pair(t):
        yy = (y + t) % NY
        rows = pmat[pl.ds(pl.multiple_of(yy * 352, 16), 352), :]
        bsend[yy] = nn(rows, grad[...]).astype(BF16).reshape(2, 176, 336)
        if t:
            o = (3 - t) % NY
            cp = rcopy(bsend.at[yy], byr.at[o], b_sem.at[0, t], b_sem.at[1, o], at_mp(yy * 2 + xh))
            cp.start()
            pending.append(cp)

    for t in (2, 1, 3, 0):
        back_pair(t)

    gz_pending = []
    for kk in order:
        rcopy(gxr.at[kk], gxr.at[kk], g_sem.at[2, kk], g_sem.at[3, kk], xpart).wait_recv()
        v = gs[kk, 2 * c + xl].astype(F32) + grecv[kk, xl].astype(F32) + gxr[kk].astype(F32)
        gzs[kk] = v.astype(BF16)
        if kk is not z:
            cp = rcopy(gzs.at[kk], gzr.at[z], g_sem.at[4, kk], g_sem.at[5, z], at_z(kk))
            cp.start()
            pending.append(cp)

    for o in range(1, NZ):
        zz = (z + o) % NZ
        rcopy(lossz.at[zz], lossz.at[zz], l_sem.at[0, o], l_sem.at[1, zz], at_z(zz)).wait_recv()
    loss = lossz[0]
    for zz in range(1, NZ):
        loss = loss + lossz[zz]
    lossx[0] = loss
    cp = rcopy(lossx.at[0], lossx.at[1], l_sem.at[2, 0], l_sem.at[2, 1], xpart)
    cp.start()
    pending.append(cp)

    for o in range(3):
        rcopy(byr.at[o], byr.at[o], b_sem.at[0, 0], b_sem.at[1, o], xhpart).wait_recv()

    def back_sum(j):
        v = bsend[y, j].astype(F32)
        for o in range(3):
            v = v + byr[o, j].astype(F32)
        return v

    bxs[...] = back_sum(1 - xh).astype(BF16)
    bcp = rcopy(bxs, bxr, b_sem.at[2, 0], b_sem.at[2, 1], xhpart)
    bcp.start()
    pending.append(bcp)

    total = gzs[z].astype(F32)
    for o in range(1, NZ):
        zz = (z + o) % NZ
        rcopy(gzr.at[zz], gzr.at[zz], g_sem.at[4, zz], g_sem.at[5, zz], at_z(zz)).wait_recv()
        total = total + gzr[zz].astype(F32)
    q_own = 2 * c + xl
    q_x = 2 * c + 1 - xl
    ag[z, q_own] = (total * (head_scale / token_total)).astype(BF16)

    def ag_send(ref, ssem, rsem, device):
        cp = rcopy(ref, ref, ssem, rsem, device)
        cp.start()
        pending.append(cp)

    def ag_z(ref, sid, rsem, off):
        ag_send(ref, agz_sem.at[0, sid], rsem, at_z((z + off + NZ) % NZ))

    mine = ag.at[z, q_own]
    ag_z(mine, 0, agz_sem.at[1, z], 1)
    ag_z(mine, 1, agz_sem.at[1, z], -1)
    ag_send(mine, agx_sem.at[0, z], agx_sem.at[1, z], xpart)
    ag_z(mine, 2, agz_sem.at[1, z], 2)
    ag_z(mine, 3, agz_sem.at[1, z], -2)
    ag_send(mine, agp_sem.at[0, z, xl], agp_sem.at[1, z, xl], pair)

    rcopy(lossx.at[0], lossx.at[1], l_sem.at[2, 0], l_sem.at[2, 1], xpart).wait_recv()
    lossc[0] = lossx[0] + lossx[1]
    cp = rcopy(lossc.at[0], lossc.at[1], l_sem.at[3, 0], l_sem.at[3, 1], pair)
    cp.start()
    pending.append(cp)
    bcp.wait_recv()
    v = back_sum(xh) + bxr[...].astype(F32)
    for i in range(3):
        bfin[i] = v[:, 112 * i : 112 * i + 112]
    back_store = pltpu.make_async_copy(bfin, back_out, out_sem.at[2])
    back_store.start()

    def from_z(off):
        zz = (z + off + NZ) % NZ
        ref = ag.at[zz, q_own]
        rcopy(ref, ref, agz_sem.at[0, 0], agz_sem.at[1, zz], pair).wait_recv()
        if off == -2:
            ag_z(ref, 4, agz_sem.at[1, zz], 2)
            ag_z(ref, 5, agz_sem.at[1, zz], 1)
        if off == 2:
            ag_z(ref, 6, agz_sem.at[1, zz], -1)
        if off != 1:
            ag_send(ref, agx_sem.at[0, zz], agx_sem.at[1, zz], xpart)
        ag_send(ref, agp_sem.at[0, zz, xl], agp_sem.at[1, zz, xl], pair)

    def from_x(off):
        zz = (z + off + NZ) % NZ
        ref = ag.at[zz, q_x]
        rcopy(ref, ref, agx_sem.at[0, zz], agx_sem.at[1, zz], xpart).wait_recv()
        if off == 0:
            ag_z(ref, 7, agx_sem.at[1, zz], -1)
        ag_send(ref, agp_sem.at[0, zz, 1 - xl], agp_sem.at[1, zz, 1 - xl], pair)

    from_z(-1)
    from_z(1)
    from_x(0)
    from_z(-2)
    from_z(2)
    from_x(-1)
    from_z(-3)
    from_z(3)
    from_x(1)
    from_z(-4)
    for off in (-2, 2, -3, 3, -4):
        from_x(off)

    rcopy(lossc.at[0], lossc.at[1], l_sem.at[3, 0], l_sem.at[3, 1], pair).wait_recv()
    loss_out[...] = (lossc[0, 0:1, 0:1] + lossc[1, 0:1, 0:1]) / token_total

    for zz in range(NZ):
        for x in range(2):
            ref = ag.at[zz, 2 * (1 - c) + x]
            rcopy(ref, ref, agp_sem.at[0, zz, x], agp_sem.at[1, zz, x], pair).wait_recv()
        for q in range(4):
            for j in range(13 if zz < 7 else 8):
                r, l = divmod(zz * 13 + j, 11)
                lo = 144 * q + 16 * r
                fout[lo : lo + 16, 128 * l : 128 * l + 128] = ag[zz, q, j]
    stores = [
        back_store,
        pltpu.make_async_copy(fout.at[pl.ds(0, 400)], gp6_out, out_sem.at[0]),
        pltpu.make_async_copy(fout.at[pl.ds(400, 176)], gpg_out, out_sem.at[1]),
    ]
    stores[1].start()
    stores[2].start()

    for away, descriptor in ysends:

        @pl.when(away)
        def _(descriptor=descriptor):
            descriptor().wait_send()

    for k in range(2):
        for sub in range(2):
            xh_copy(k, sub).wait_send()
    for cp in pending:
        cp.wait_send()
    for cp in stores:
        cp.wait()


def local(
    student_feats,
    keep_index,
    hidden_six,
    resid_six,
    down_six,
    hidden_giant,
    resid_giant,
    down_giant,
    proj_six,
    proj_giant,
):
    token_total = 336 * 32
    dma = pltpu.SemaphoreType.DMA
    hbm = pl.BlockSpec(memory_space=pl.ANY)
    vmem = pl.BlockSpec(memory_space=pltpu.VMEM)
    scratch = [
        pltpu.VMEM((100, 1600), BF16),
        pltpu.VMEM((44, 768), BF16),
        pltpu.VMEM((32, 112, 1664), BF16),
        pltpu.VMEM((32, 48, 768), BF16),
        pltpu.VMEM((3, 560, 1600), BF16),
        pltpu.VMEM((3, 560, 768), BF16),
        pltpu.VMEM((3, 400, 560), BF16),
        pltpu.VMEM((3, 176, 560), BF16),
        pltpu.VMEM((336, 1664), BF16),
        pltpu.VMEM((336, 768), BF16),
        pltpu.VMEM((336, 1408), BF16),
        pltpu.VMEM((576, 1408), BF16),
        pltpu.VMEM((1408, 576), BF16),
        pltpu.VMEM((32, 144, 336), BF16),
        pltpu.VMEM((2, 4, 2, 144, 336), BF16),
        pltpu.VMEM((2, 2, 144, 336), BF16),
        pltpu.VMEM((2, 2, 144, 336), BF16),
        pltpu.VMEM((48, 768), F32),
        pltpu.VMEM((16, 144, 336), BF16),
        pltpu.VMEM((576, 336), F32),
        pltpu.VMEM((576, 336), F32),
        pltpu.VMEM((8, 8, 336), F32),
        pltpu.VMEM((576, 336), BF16),
        pltpu.VMEM((NZ, 4, 13, 16, 128), BF16),
        pltpu.VMEM((NZ, 2, 13, 16, 128), BF16),
        pltpu.VMEM((NZ, 13, 16, 128), BF16),
        pltpu.VMEM((NZ, 13, 16, 128), BF16),
        pltpu.VMEM((NZ, 13, 16, 128), BF16),
        pltpu.VMEM((NZ, 13, 16, 128), BF16),
        pltpu.VMEM((NZ, 4, 13, 16, 128), BF16),
        pltpu.VMEM((576, 1408), BF16),
        pltpu.VMEM((NY, 2, 176, 336), BF16),
        pltpu.VMEM((3, 2, 176, 336), BF16),
        pltpu.VMEM((176, 336), BF16),
        pltpu.VMEM((176, 336), BF16),
        pltpu.VMEM((3, 176, 112), F32),
        pltpu.VMEM((NZ, 8, 128), F32),
        pltpu.VMEM((2, 8, 128), F32),
        pltpu.VMEM((2, 8, 128), F32),
        dma((9,)),
        dma((3, 15)),
        dma((3, 15)),
        dma((3, 16)),
        dma((3, 16)),
        dma((2, 16, 2)),
        dma((2, 2, 4, 2)),
        dma((2, 16)),
        dma((2, 2, 2)),
        dma((2, 8)),
        dma((6, 8)),
        dma((3, 8)),
        dma((2, 8)),
        dma((2, 8, 2)),
        dma((3, 4)),
        dma((4, 8)),
        dma((3,)),
    ]
    gp6, gpg, back, loss = pl.pallas_call(
        functools.partial(kernel, token_total),
        out_shape=(
            jax.ShapeDtypeStruct((400, 1408), BF16),
            jax.ShapeDtypeStruct((176, 1408), BF16),
            jax.ShapeDtypeStruct((3, 176, 112), F32),
            jax.ShapeDtypeStruct((1, 1), F32),
        ),
        in_specs=[vmem] + [hbm] * 9,
        out_specs=(hbm, hbm, hbm, vmem),
        scratch_shapes=scratch,
        compiler_params=pltpu.CompilerParams(
            collective_id=0, has_side_effects=True, vmem_limit_bytes=62 * 1024 * 1024
        ),
        cost_estimate=pl.CostEstimate(flops=6_000_000_000, bytes_accessed=20_000_000, transcendentals=0),
    )(
        keep_index,
        student_feats.reshape(336, 1408),
        hidden_six,
        resid_six.transpose(0, 2, 1),
        down_six.T,
        hidden_giant,
        resid_giant.transpose(0, 2, 1),
        down_giant.T,
        proj_six.T,
        proj_giant.T,
    )
    return (back.transpose(0, 2, 1), gp6.astype(F32).T, gpg.astype(F32).T, loss.reshape(()))


def solution(mesh):
    return jax.shard_map(
        local,
        mesh=mesh,
        in_specs=(
            P("dp", None, None),
            P("dp", None),
            P("dp", None, "mp"),
            P("dp", None, "mp"),
            P("mp", "dp"),
            P("dp", None, "mp"),
            P("dp", None, "mp"),
            P("mp", "dp"),
            P(None, "mp"),
            P(None, "mp"),
        ),
        out_specs=(P("dp", None, "mp"), P(None, "mp"), P(None, "mp"), P()),
        check_vma=False,
    )
```

```python
import functools

import jax
import jax.numpy as jnp
from jax import lax
from jax.experimental import pallas as pl
from jax.experimental.pallas import tpu as pltpu
from jax.sharding import PartitionSpec as P

loss_scale = 256.0
head_scale = 64.0
norm_eps = 1e-06

NZ = 8
NY = 4
F32 = jnp.float32
BF16 = jnp.bfloat16
MESH = pl.DeviceIdType.MESH

SENDS = (
    ((0, 0), (0, 0), (0, 0)),
    ((0, -1), (0, 1), (0, -1)),
    ((0, -2), (0, 2), (0, -2)),
    ((0, -3), (1, 0), (0, 3)),
    ((1, -2), (1, 1), (0, 4)),
)
RECVS = (
    ((0, -1), (0, 1), (1, 0)),
    ((0, -2), (0, 2), (1, -1)),
    ((0, -3), (0, 3), (1, -2)),
    ((0, -4), (1, 1), (1, 3)),
    ((1, -3), (1, 2), (1, 4)),
)
STEPS = len(SENDS)
OWN = 3 * STEPS


def nt(a, b):
    return lax.dot_general(a, b, (((1,), (1,)), ((), ())), preferred_element_type=F32)


def nn(a, b):
    return lax.dot_general(a, b, (((1,), (0,)), ((), ())), preferred_element_type=F32)


def kernel(
    token_total,
    keep_hbm,
    stu_hbm,
    h6_hbm,
    r6_hbm,
    w6_hbm,
    hg_hbm,
    rg_hbm,
    wg_hbm,
    p6_hbm,
    pg_hbm,
    gp6_out,
    gpg_out,
    back_out,
    loss_out,
    keep,
    w6_in,
    wg_in,
    gath6,
    gathg,
    h6,
    hg,
    r6,
    rg,
    rows6,
    rowsg,
    stu,
    pt,
    pmat,
    part,
    yrecv,
    xsend,
    xrecv,
    wpad,
    yrel,
    tgt,
    outs,
    stats,
    grad,
    gs,
    grecv,
    gxs,
    gxr,
    gzs,
    gzr,
    ag,
    fout,
    bsend,
    byr,
    bxs,
    bxr,
    bfin,
    lossz,
    lossx,
    lossc,
    lossv,
    load_sem,
    wsend_sem,
    wrecv_sem,
    psend_sem,
    precv_sem,
    ysend_sem,
    yrecv_sem,
    yrel_sem,
    xh_sem,
    st_sem,
    g_sem,
    agz_sem,
    agx_sem,
    agp_sem,
    b_sem,
    l_sem,
    out_sem,
):
    dp = lax.axis_index("dp")
    mp = lax.axis_index("mp")
    c = dp % 2
    z = (dp // 2) % NZ
    xl = dp // (2 * NZ)
    y = mp // 2
    xh = mp % 2

    pair = {"dp": dp + 1 - 2 * c}
    xpart = {"dp": (1 - xl) * 2 * NZ + z * 2 + c}
    xhpart = {"mp": y * 2 + 1 - xh}

    def at_z(zz):
        return {"dp": xl * 2 * NZ + zz * 2 + c}

    def at_mp(m):
        return {"mp": m}

    zup = at_z((z + 1) % NZ)
    yup = at_mp(((y + 1) % NY) * 2 + xh)
    ydown = at_mp(((y + NY - 1) % NY) * 2 + xh)
    zdown = at_z((z + NZ - 1) % NZ)

    def rcopy(src, dst, ssem, rsem, device):
        return pltpu.make_async_remote_copy(
            src_ref=src, dst_ref=dst, send_sem=ssem, recv_sem=rsem, device_id=device, device_id_type=MESH
        )

    barrier = pltpu.get_barrier_semaphore()
    peers = [pair, xpart]
    peers += [at_z((z + o) % NZ) for o in range(1, NZ)]
    peers += [at_mp((mp + o) % 8) for o in range(1, 8)]
    for device in peers:
        pl.semaphore_signal(barrier, inc=1, device_id=device, device_id_type=MESH)

    loads = [
        pltpu.make_async_copy(src, dst, load_sem.at[i])
        for i, (src, dst) in enumerate(
            (
                (w6_hbm, w6_in),
                (wg_hbm, wg_in),
                (h6_hbm, h6),
                (hg_hbm, hg),
                (stu_hbm, stu),
                (p6_hbm, pt.at[pl.ds(0, 400)]),
                (pg_hbm, pt.at[pl.ds(400, 176)]),
                (r6_hbm, r6),
                (rg_hbm, rg),
                (keep_hbm, keep),
            )
        )
    ]
    for load in loads[:2]:
        load.start()

    def slot_of(block):
        plane, off = block
        pl_ = xl if plane == 0 else 1 - xl
        return pl_ * 2 * NZ + ((z + off + NZ) % NZ) * 2

    def piece(p, slot):
        if p == 0:
            return gath6.at[slot, pl.ds(0, 80)]
        if p == 1:
            return gath6.at[slot, pl.ds(80, 32)]
        return gathg.at[slot]

    wtargets = (zup, zdown, xpart)
    pending = []

    def send_w(s, k, p):
        ref = piece(p, slot_of(SENDS[s][k]) + c)
        cp = rcopy(ref, ref, wsend_sem.at[p, 3 * s + k], wrecv_sem.at[p, 3 * s + k], wtargets[k])
        cp.start()
        pending.append(cp)

    def send_pair(unit, block, p):
        ref = piece(p, slot_of(block) + c)
        cp = rcopy(ref, ref, psend_sem.at[p, unit], precv_sem.at[p, unit], pair)
        cp.start()
        pending.append(cp)

    def wait_w(s, k, p):
        ref = piece(p, slot_of(RECVS[s][k]) + c)
        rcopy(ref, ref, wsend_sem.at[p, 3 * s + k], wrecv_sem.at[p, 3 * s + k], wtargets[k]).wait_recv()

    own = dp
    loads[0].wait()
    gath6[own, 96:112, :] = jnp.zeros((16, 1664), BF16)
    gath6[own, 0:96, 1536:1664] = jnp.zeros((96, 128), BF16)
    gath6[own, 0:100, 0:1600] = w6_in[...]
    pl.semaphore_wait(barrier, len(peers))
    for p in range(2):
        for k in range(3):
            send_w(0, k, p)
    loads[1].wait()
    wpad[0:4, :] = jnp.zeros((4, 768), F32)
    wpad[4:48, :] = wg_in[...].astype(F32)
    gathg[own] = wpad[...].astype(BF16)
    for k in range(3):
        send_w(0, k, 2)
    for p in range(3):
        send_pair(OWN, (0, 0), p)
    for load in loads[2:]:
        load.start()

    def column(row):
        a = lax.broadcasted_iota(jnp.int32, (112, 112), 0)
        b = lax.broadcasted_iota(jnp.int32, (112, 112), 1)
        return jnp.sum(jnp.where(a == b, row.astype(F32), 0.0), axis=1, keepdims=True)

    rows6[:, 1536:1664] = jnp.zeros((336, 128), BF16)
    def pick_rows(i):
        lane = lax.broadcasted_iota(jnp.int32, (112, 560), 1).astype(F32)
        pick = (column(keep[i : i + 1, :]) == lane).astype(F32).astype(BF16)
        rows6[112 * i : 112 * i + 112, 0:1600] = nn(pick, h6[i]).astype(BF16)
        rowsg[112 * i : 112 * i + 112, :] = nn(pick, hg[i]).astype(BF16)

    loads[2].wait()
    loads[3].wait()
    loads[9].wait()
    pick_rows(0)
    pick_rows(1)

    ysends = []
    relays = []

    SUBS = ((0, 80), (80, 64))

    def compute(items, sub):
        slots = [slot_of(block) for unit, block in items]
        for (unit, block), slot in zip(items, slots):
            for p in ((0,), (1, 2))[sub]:
                ref = piece(p, slot + 1 - c)
                rcopy(ref, ref, psend_sem.at[p, unit], precv_sem.at[p, unit], pair).wait_recv()

        def rows_of(ref, lo, hi):
            blocks = [ref[pl.ds(slot, 2), lo:hi].reshape(2 * (hi - lo), ref.shape[2]) for slot in slots]
            return jnp.concatenate(blocks, axis=0)

        if sub == 0:
            six = nt(rows_of(gath6, 0, 80), rows6[...]).astype(BF16)
            for i, slot in enumerate(slots):
                part[pl.ds(slot, 2), 0:80, :] = six[160 * i : 160 * i + 160].reshape(2, 80, 336)
        else:
            six = nt(rows_of(gath6, 80, 112), rows6[...])
            giant = nt(rows_of(gathg, 0, 48), rowsg[...])
            for i, slot in enumerate(slots):
                for cc in range(2):
                    a = six[64 * i + 32 * cc : 64 * i + 32 * cc + 32]
                    b = giant[96 * i + 48 * cc : 96 * i + 48 * cc + 48]
                    part[slot + cc, 80:96, :] = a[0:16].astype(BF16)
                    part[slot + cc, 96:112, :] = (a[16:32] + b[0:16]).astype(BF16)
                    part[slot + cc, 112:144, :] = b[16:48].astype(BF16)
        for (unit, block), slot in zip(items, slots):
            pass_round(unit, slot, sub)

    def pass_round(unit, slot, sub):
        lo, n = SUBS[sub]
        role = (y - slot // 8 + NY) % NY
        u = (slot // 2) % 4
        rows = pl.ds(lo, n)

        def send(cond, src, dst, ssem, rsem, device):
            @pl.when(cond)
            def _():
                rcopy(src, dst, ssem, rsem, device).start()

            ysends.append((cond, lambda: rcopy(src, dst, ssem, rsem, device)))

        first, second = part.at[slot, rows], part.at[slot + 1, rows]
        rel, rsem = yrel.at[unit, rows], yrel_sem.at[sub, unit]
        s0, s1 = ysend_sem.at[sub, unit, 0], ysend_sem.at[sub, unit, 1]
        send(role == 2, first, rel, s0, rsem, ydown)
        send(role == 2, second, rel, s1, rsem, yup)
        send(role == 1, second, yrecv.at[0, u, 1, rows], s0, yrecv_sem.at[sub, 0, u, 1], ydown)
        send(role == 3, first, yrecv.at[1, u, 0, rows], s0, yrecv_sem.at[sub, 1, u, 0], yup)

        def relay():
            for want, cc, side, device in ((1, 0, 0, ydown), (3, 1, 1, yup)):

                def descriptor(cc=cc, side=side, device=device):
                    dst = yrecv.at[side, u, cc, rows]
                    return rcopy(part.at[slot + cc, rows], dst, s1, yrecv_sem.at[sub, side, u, cc], device)

                @pl.when(role == want)
                def _(cc=cc, device=device, descriptor=descriptor):
                    rcopy(rel, rel, s1, rsem, device).wait_recv()
                    both = part[slot + cc, lo : lo + n].astype(F32) + yrel[unit, lo : lo + n].astype(F32)
                    part[slot + cc, lo : lo + n] = both.astype(BF16)
                    descriptor().start()

                ysends.append((role == want, descriptor))

        relays.append(relay)

    def head_out(i):
        if i == 0:
            for load in loads[4:9]:
                load.wait()
        outs[192 * i : 192 * i + 192, :] = nt(pt[192 * i : 192 * i + 192, :], stu[...])

    def turn_heads(lo, hi):
        for l in range(lo, hi):
            pmat[128 * l : 128 * l + 128, :] = pt[:, 128 * l : 128 * l + 128].T

    def residuals(i):
        row = jnp.concatenate([keep[j : j + 1, :] for j in range(3)], axis=1)
        pos = lax.broadcasted_iota(jnp.int32, (560, 336), 0)
        col = lax.broadcasted_iota(jnp.int32, (560, 336), 1)
        clip = (col >= 112 * i) & (col < 112 * i + 112)
        pick = ((row == pos) & clip).astype(F32).astype(BF16)
        a = nn(r6[i], pick)
        b = nn(rg[i], pick)
        if i == 0:
            tgt[0:400, :] = a
            tgt[400:576, :] = b
        else:
            tgt[0:400, :] += a
            tgt[400:576, :] += b

    work = [functools.partial(head_out, i) for i in range(3)]
    work += [functools.partial(residuals, i) for i in range(3)]
    work += [functools.partial(turn_heads, 0, 6), functools.partial(turn_heads, 6, 11)]

    def step_units(s):
        return [(3 * s + k, RECVS[s][k]) for k in range(3)]

    def run_relays(keep_back):
        while len(relays) > keep_back:
            relays.pop(0)()

    for s in range(STEPS):
        for ps in ((0,), (1, 2)):
            for p in ps:
                for k in range(3):
                    wait_w(s, k, p)
                if s + 1 < STEPS:
                    for k in range(3):
                        send_w(s + 1, k, p)
                for k in range(3):
                    send_pair(3 * s + k, RECVS[s][k], p)
            if ps == (0,):
                if s == 0:
                    pick_rows(2)
                    compute([(OWN, (0, 0))], 0)
                    compute([(OWN, (0, 0))], 1)
                else:
                    compute(step_units(s - 1), 1)
                run_relays(3)
                compute(step_units(s), 0)
            elif s + 1 < STEPS:
                work.pop(0)()
                work.pop(0)()
                run_relays(3)

    def summed(u, cc, sub):
        lo, n = SUBS[sub]
        total = part[y * 8 + u * 2 + cc, lo : lo + n].astype(F32)
        for side in range(2):
            total = total + yrecv[side, u, cc, lo : lo + n].astype(F32)
        return total

    def wait_y(u, sub):
        for side in range(2):
            for cc in range(2):
                ref = yrecv.at[side, u, cc, pl.ds(*SUBS[sub])]
                rcopy(ref, ref, ysend_sem.at[0, 0, 0], yrecv_sem.at[sub, side, u, cc], xhpart).wait_recv()

    def xh_copy(k, sub):
        rows = pl.ds(*SUBS[sub])
        src, dst = xsend.at[k, pl.ds(0, 2), rows], xrecv.at[k, pl.ds(0, 2), rows]
        return rcopy(src, dst, xh_sem.at[0, k, sub], xh_sem.at[1, k, sub], xhpart)

    def exchange(sub):
        lo, n = SUBS[sub]
        for k in range(2):
            u = 2 * (1 - xh) + k
            wait_y(u, sub)
            for cc in range(2):
                xsend[k, cc, lo : lo + n] = summed(u, cc, sub).astype(BF16)
            xh_copy(k, sub).start()

    def targets(sub):
        for k in range(2):
            u = 2 * xh + k
            wait_y(u, sub)
            xh_copy(k, sub).wait_recv()
            lo, n = SUBS[sub]
            for cc in range(2):
                total = summed(u, cc, sub) + xrecv[k, cc, lo : lo + n].astype(F32)
                f = 100 * (2 * k + cc)
                if sub == 0:
                    tgt[f : f + 80, :] += total
                else:
                    tgt[f + 80 : f + 100, :] += total[0:20]
                    f = 400 + 44 * (2 * k + cc)
                    tgt[f : f + 44, :] += total[20:64]

    early = y // 2 == xl

    run_relays(0)
    compute(step_units(STEPS - 1), 1)
    exchange(0)
    pl.when(early)(functools.partial(exchange, 1))
    run_relays(0)
    pl.when(jnp.logical_not(early))(functools.partial(exchange, 1))
    targets(0)
    targets(1)

    def sums(lo, hi):
        t = tgt[lo:hi, :]
        o = outs[lo:hi, :]
        return [
            jnp.sum(o * t, axis=0, keepdims=True),
            jnp.sum(o * o, axis=0, keepdims=True),
            jnp.sum(t * t, axis=0, keepdims=True),
        ]

    for i, row in enumerate(sums(0, 400) + sums(400, 576)):
        stats[mp, i : i + 1, :] = row
    for i in range(6, 8):
        stats[mp, i : i + 1, :] = jnp.zeros((1, 336), F32)
    st = []
    for o in range(1, 8):
        m = (mp + o) % 8
        cp = rcopy(stats.at[mp], stats.at[mp], st_sem.at[0, o], st_sem.at[1, mp], at_mp(m))
        cp.start()
        pending.append(cp)
    for o in range(1, 8):
        m = (mp + o) % 8
        rcopy(stats.at[m], stats.at[m], st_sem.at[0, o], st_sem.at[1, m], at_mp(m)).wait_recv()
    total = stats[0]
    for m in range(1, 8):
        total = total + stats[m]

    def gradient(lo, hi, i):
        norm_out = jnp.sqrt(total[i + 1 : i + 2] + norm_eps)
        norm_tar = jnp.sqrt(total[i + 2 : i + 3] + norm_eps)
        both = norm_out * norm_tar
        cosine = total[i : i + 1] / both
        a = -loss_scale / both
        b = loss_scale * cosine / (norm_out * norm_out)
        grad[lo:hi, :] = (tgt[lo:hi, :] * a + outs[lo:hi, :] * b).astype(BF16)
        return cosine

    cos6 = gradient(0, 400, 0)
    cosg = gradient(400, 576, 3)
    loss_local = jnp.sum(2.0 - cos6 - cosg, axis=1, keepdims=True)
    lossz[z] = jnp.broadcast_to(loss_local, (8, 128))
    for o in range(1, NZ):
        zz = (z + o) % NZ
        cp = rcopy(lossz.at[z], lossz.at[z], l_sem.at[0, o], l_sem.at[1, z], at_z(zz))
        cp.start()
        pending.append(cp)

    offsets = (-4, -3, 3, 1, -2, 2, -1, 0)
    at = {off: (z + off + NZ) % NZ for off in offsets}

    def head_rows(core):
        rows = grad[pl.ds(pl.multiple_of(core * 288, 16), 288), :]
        g = nn(rows, stu[...]).astype(BF16)
        for x in range(2):
            for r in range(9):
                for l in range(11):
                    t = r * 11 + l
                    lo = 144 * x + 16 * r
                    gs[t // 13, 2 * core + x, t % 13] = g[lo : lo + 16, 128 * l : 128 * l + 128]
            for j in range(8, 13):
                gs[7, 2 * core + x, j] = jnp.zeros((16, 128), BF16)

    head_rows(1 - c)
    for kk in at.values():
        cp = rcopy(gs.at[kk, pl.ds(2 * (1 - c), 2)], grecv.at[kk], g_sem.at[0, kk], g_sem.at[1, kk], pair)
        cp.start()
        pending.append(cp)
    head_rows(c)

    def both_cores(kk, x):
        return gs[kk, 2 * c + x].astype(F32) + grecv[kk, x].astype(F32)

    def to_x(kk):
        cp = rcopy(gxs.at[kk], gxr.at[kk], g_sem.at[2, kk], g_sem.at[3, kk], xpart)
        cp.start()
        pending.append(cp)

    def z_hop(src, sid, step):
        cp = rcopy(src, gzr.at[sid], g_sem.at[4, sid], g_sem.at[5, sid], at_z((z + step + NZ) % NZ))
        cp.start()
        pending.append(cp)

    def from_hop(sid):
        rcopy(gzr.at[sid], gzr.at[sid], g_sem.at[4, sid], g_sem.at[5, sid], pair).wait_recv()
        return gzr[sid].astype(F32)

    for off, kk in at.items():
        rcopy(grecv.at[kk], grecv.at[kk], g_sem.at[0, kk], g_sem.at[1, kk], pair).wait_recv()
        if off:
            gxs[kk] = both_cores(kk, 1 - xl).astype(BF16)
            if off == 1:
                z_hop(gxs.at[kk], 7, 1)
            else:
                to_x(kk)

    def back_pair(t):
        yy = (y + t) % NY
        rows = pmat[pl.ds(pl.multiple_of(yy * 352, 16), 352), :]
        bsend[yy] = nn(rows, grad[...]).astype(BF16).reshape(2, 176, 336)
        if t:
            o = (3 - t) % NY
            cp = rcopy(bsend.at[yy], byr.at[o], b_sem.at[0, t], b_sem.at[1, o], at_mp(yy * 2 + xh))
            cp.start()
            pending.append(cp)

    def own_part(off):
        kk = at[off]
        v = both_cores(kk, xl)
        if off != 1:
            rcopy(gxr.at[kk], gxr.at[kk], g_sem.at[2, kk], g_sem.at[3, kk], xpart).wait_recv()
            v = v + gxr[kk].astype(F32)
        return v

    def pass_on(off, value, sid, step):
        gzs[at[off]] = value.astype(BF16)
        z_hop(gzs.at[at[off]], sid, step)

    pass_on(1, own_part(1), 4, 1)
    back_pair(2)
    back_pair(1)
    gxs[z] = (both_cores(z, 1 - xl) + from_hop(7)).astype(BF16)
    to_x(z)
    pass_on(-4, own_part(-4), 0, -2)
    pass_on(-3, own_part(-3), 1, -1)
    pass_on(3, own_part(3), 2, 1)
    back_pair(3)
    back_pair(0)
    pass_on(-2, own_part(-2) + from_hop(0) + from_hop(1), 5, -2)
    pass_on(2, own_part(2) + from_hop(2), 6, 2)
    pass_on(-1, own_part(-1), 3, -1)

    for o in range(1, NZ):
        zz = (z + o) % NZ
        rcopy(lossz.at[zz], lossz.at[zz], l_sem.at[0, o], l_sem.at[1, zz], at_z(zz)).wait_recv()
    loss = lossz[0]
    for zz in range(1, NZ):
        loss = loss + lossz[zz]
    lossx[0] = loss
    cp = rcopy(lossx.at[0], lossx.at[1], l_sem.at[2, 0], l_sem.at[2, 1], xpart)
    cp.start()
    pending.append(cp)

    for o in range(3):
        rcopy(byr.at[o], byr.at[o], b_sem.at[0, 0], b_sem.at[1, o], xhpart).wait_recv()

    def back_sum(j):
        v = bsend[y, j].astype(F32)
        for o in range(3):
            v = v + byr[o, j].astype(F32)
        return v

    bxs[...] = back_sum(1 - xh).astype(BF16)
    bcp = rcopy(bxs, bxr, b_sem.at[2, 0], b_sem.at[2, 1], xhpart)
    bcp.start()
    pending.append(bcp)

    total = own_part(0)
    for sid in (4, 3, 6, 5):
        total = total + from_hop(sid)
    q_own = 2 * c + xl
    q_x = 2 * c + 1 - xl
    ag[z, q_own] = (total * (head_scale / token_total)).astype(BF16)

    def ag_send(ref, ssem, rsem, device):
        cp = rcopy(ref, ref, ssem, rsem, device)
        cp.start()
        pending.append(cp)

    def ag_z(ref, sid, rsem, off):
        ag_send(ref, agz_sem.at[0, sid], rsem, at_z((z + off + NZ) % NZ))

    mine = ag.at[z, q_own]
    ag_z(mine, 0, agz_sem.at[1, z], 1)
    ag_z(mine, 1, agz_sem.at[1, z], -1)
    ag_send(mine, agx_sem.at[0, z], agx_sem.at[1, z], xpart)
    ag_z(mine, 2, agz_sem.at[1, z], 2)
    ag_z(mine, 3, agz_sem.at[1, z], -2)
    ag_send(mine, agp_sem.at[0, z, xl], agp_sem.at[1, z, xl], pair)

    def from_z(off):
        zz = (z + off + NZ) % NZ
        ref = ag.at[zz, q_own]
        rcopy(ref, ref, agz_sem.at[0, 0], agz_sem.at[1, zz], pair).wait_recv()
        if off == -2:
            ag_z(ref, 4, agz_sem.at[1, zz], 2)
            ag_z(ref, 5, agz_sem.at[1, zz], 1)
        if off == 2:
            ag_z(ref, 6, agz_sem.at[1, zz], -1)
        if off != 1:
            ag_send(ref, agx_sem.at[0, zz], agx_sem.at[1, zz], xpart)
        ag_send(ref, agp_sem.at[0, zz, xl], agp_sem.at[1, zz, xl], pair)

    def from_x(off):
        zz = (z + off + NZ) % NZ
        ref = ag.at[zz, q_x]
        rcopy(ref, ref, agx_sem.at[0, zz], agx_sem.at[1, zz], xpart).wait_recv()
        if off == 0:
            ag_z(ref, 7, agx_sem.at[1, zz], -1)
        ag_send(ref, agp_sem.at[0, zz, 1 - xl], agp_sem.at[1, zz, 1 - xl], pair)

    from_z(-1)
    from_z(1)
    from_x(0)
    from_z(-2)
    from_z(2)

    rcopy(lossx.at[0], lossx.at[1], l_sem.at[2, 0], l_sem.at[2, 1], xpart).wait_recv()
    lossc[0] = lossx[0] + lossx[1]
    cp = rcopy(lossc.at[0], lossc.at[1], l_sem.at[3, 0], l_sem.at[3, 1], pair)
    cp.start()
    pending.append(cp)
    bcp.wait_recv()
    v = back_sum(xh) + bxr[...].astype(F32)
    for i in range(3):
        bfin[i] = v[:, 112 * i : 112 * i + 112]
    back_store = pltpu.make_async_copy(bfin, back_out, out_sem.at[2])
    back_store.start()

    from_x(-1)
    from_z(-3)
    from_z(3)
    rcopy(lossc.at[0], lossc.at[1], l_sem.at[3, 0], l_sem.at[3, 1], pair).wait_recv()
    lossv[...] = (lossc[0, 0:1, 0:1] + lossc[1, 0:1, 0:1]) / token_total
    loss_store = pltpu.make_async_copy(lossv, loss_out, out_sem.at[3])
    loss_store.start()
    from_x(1)
    from_z(-4)
    for off in (-2, 2, -3, 3, -4):
        from_x(off)

    for zz in range(NZ):
        for x in range(2):
            ref = ag.at[zz, 2 * (1 - c) + x]
            rcopy(ref, ref, agp_sem.at[0, zz, x], agp_sem.at[1, zz, x], pair).wait_recv()
        for q in range(4):
            for j in range(13 if zz < 7 else 8):
                r, l = divmod(zz * 13 + j, 11)
                lo = 144 * q + 16 * r
                fout[lo : lo + 16, 128 * l : 128 * l + 128] = ag[zz, q, j]
    stores = [
        back_store,
        loss_store,
        pltpu.make_async_copy(fout.at[pl.ds(0, 400)], gp6_out, out_sem.at[0]),
        pltpu.make_async_copy(fout.at[pl.ds(400, 176)], gpg_out, out_sem.at[1]),
    ]
    stores[2].start()
    stores[3].start()

    for away, descriptor in ysends:

        @pl.when(away)
        def _(descriptor=descriptor):
            descriptor().wait_send()

    for k in range(2):
        for sub in range(2):
            xh_copy(k, sub).wait_send()
    for cp in pending:
        cp.wait_send()
    for cp in stores:
        cp.wait()


def local(
    student_feats,
    keep_index,
    hidden_six,
    resid_six,
    down_six,
    hidden_giant,
    resid_giant,
    down_giant,
    proj_six,
    proj_giant,
):
    token_total = 336 * 32
    dma = pltpu.SemaphoreType.DMA
    hbm = pl.BlockSpec(memory_space=pl.ANY)
    scratch = [
        pltpu.VMEM((3, 112), jnp.int32),
        pltpu.VMEM((100, 1600), BF16),
        pltpu.VMEM((44, 768), BF16),
        pltpu.VMEM((32, 112, 1664), BF16),
        pltpu.VMEM((32, 48, 768), BF16),
        pltpu.VMEM((3, 560, 1600), BF16),
        pltpu.VMEM((3, 560, 768), BF16),
        pltpu.VMEM((3, 400, 560), BF16),
        pltpu.VMEM((3, 176, 560), BF16),
        pltpu.VMEM((336, 1664), BF16),
        pltpu.VMEM((336, 768), BF16),
        pltpu.VMEM((336, 1408), BF16),
        pltpu.VMEM((576, 1408), BF16),
        pltpu.VMEM((1408, 576), BF16),
        pltpu.VMEM((32, 144, 336), BF16),
        pltpu.VMEM((2, 4, 2, 144, 336), BF16),
        pltpu.VMEM((2, 2, 144, 336), BF16),
        pltpu.VMEM((2, 2, 144, 336), BF16),
        pltpu.VMEM((48, 768), F32),
        pltpu.VMEM((16, 144, 336), BF16),
        pltpu.VMEM((576, 336), F32),
        pltpu.VMEM((576, 336), F32),
        pltpu.VMEM((8, 8, 336), F32),
        pltpu.VMEM((576, 336), BF16),
        pltpu.VMEM((NZ, 4, 13, 16, 128), BF16),
        pltpu.VMEM((NZ, 2, 13, 16, 128), BF16),
        pltpu.VMEM((NZ, 13, 16, 128), BF16),
        pltpu.VMEM((NZ, 13, 16, 128), BF16),
        pltpu.VMEM((NZ, 13, 16, 128), BF16),
        pltpu.VMEM((NZ, 13, 16, 128), BF16),
        pltpu.VMEM((NZ, 4, 13, 16, 128), BF16),
        pltpu.VMEM((576, 1408), BF16),
        pltpu.VMEM((NY, 2, 176, 336), BF16),
        pltpu.VMEM((3, 2, 176, 336), BF16),
        pltpu.VMEM((176, 336), BF16),
        pltpu.VMEM((176, 336), BF16),
        pltpu.VMEM((3, 176, 112), F32),
        pltpu.VMEM((NZ, 8, 128), F32),
        pltpu.VMEM((2, 8, 128), F32),
        pltpu.VMEM((2, 8, 128), F32),
        pltpu.VMEM((1, 1), F32),
        dma((10,)),
        dma((3, 15)),
        dma((3, 15)),
        dma((3, 16)),
        dma((3, 16)),
        dma((2, 16, 2)),
        dma((2, 2, 4, 2)),
        dma((2, 16)),
        dma((2, 2, 2)),
        dma((2, 8)),
        dma((6, 8)),
        dma((3, 8)),
        dma((2, 8)),
        dma((2, 8, 2)),
        dma((3, 4)),
        dma((4, 8)),
        dma((4,)),
    ]
    gp6, gpg, back, loss = pl.pallas_call(
        functools.partial(kernel, token_total),
        out_shape=(
            jax.ShapeDtypeStruct((400, 1408), BF16),
            jax.ShapeDtypeStruct((176, 1408), BF16),
            jax.ShapeDtypeStruct((3, 176, 112), F32),
            jax.ShapeDtypeStruct((1, 1), F32),
        ),
        in_specs=[hbm] * 10,
        out_specs=(hbm, hbm, hbm, hbm),
        scratch_shapes=scratch,
        compiler_params=pltpu.CompilerParams(
            collective_id=0, has_side_effects=True, vmem_limit_bytes=62 * 1024 * 1024
        ),
        cost_estimate=pl.CostEstimate(flops=6_000_000_000, bytes_accessed=20_000_000, transcendentals=0),
    )(
        keep_index,
        student_feats.reshape(336, 1408),
        hidden_six,
        resid_six.transpose(0, 2, 1),
        down_six.T,
        hidden_giant,
        resid_giant.transpose(0, 2, 1),
        down_giant.T,
        proj_six.T,
        proj_giant.T,
    )
    return (back.transpose(0, 2, 1), gp6.astype(F32).T, gpg.astype(F32).T, loss.reshape(()))


def solution(mesh):
    return jax.shard_map(
        local,
        mesh=mesh,
        in_specs=(
            P("dp", None, None),
            P("dp", None),
            P("dp", None, "mp"),
            P("dp", None, "mp"),
            P("mp", "dp"),
            P("dp", None, "mp"),
            P("dp", None, "mp"),
            P("mp", "dp"),
            P(None, "mp"),
            P(None, "mp"),
        ),
        out_specs=(P("dp", None, "mp"), P(None, "mp"), P(None, "mp"), P()),
        check_vma=False,
    )
```

```python
import functools

import jax
import jax.numpy as jnp
from jax import lax
from jax.experimental import pallas as pl
from jax.experimental.pallas import tpu as pltpu
from jax.sharding import PartitionSpec as P

loss_scale = 256.0
head_scale = 64.0
norm_eps = 1e-06

NZ = 8
NY = 4
F32 = jnp.float32
BF16 = jnp.bfloat16
MESH = pl.DeviceIdType.MESH

SENDS = (
    ((0, 0), (0, 0), (0, 0)),
    ((0, -1), (0, 1), (0, -1)),
    ((0, -2), (0, 2), (0, -2)),
    ((0, -3), (1, 0), (0, 3)),
    ((1, -2), (1, 1), (0, 4)),
)
RECVS = (
    ((0, -1), (0, 1), (1, 0)),
    ((0, -2), (0, 2), (1, -1)),
    ((0, -3), (0, 3), (1, -2)),
    ((0, -4), (1, 1), (1, 3)),
    ((1, -3), (1, 2), (1, 4)),
)
STEPS = len(SENDS)
OWN = 3 * STEPS


def nt(a, b):
    return lax.dot_general(a, b, (((1,), (1,)), ((), ())), preferred_element_type=F32)


def nn(a, b):
    return lax.dot_general(a, b, (((1,), (0,)), ((), ())), preferred_element_type=F32)


def kernel(
    token_total,
    keep_hbm,
    stu_hbm,
    h6_hbm,
    r6_hbm,
    w6_hbm,
    hg_hbm,
    rg_hbm,
    wg_hbm,
    p6_hbm,
    pg_hbm,
    gp6_out,
    gpg_out,
    back_out,
    loss_out,
    keep,
    w6_in,
    wg_in,
    gath6,
    gathg,
    h6,
    hg,
    r6,
    rg,
    rows6,
    rowsg,
    stu,
    pt,
    pmat,
    part,
    yrecv,
    xsend,
    xrecv,
    wpad,
    yrel,
    tgt,
    outs,
    stats,
    grad,
    gs,
    grecv,
    gxs,
    gxr,
    gzs,
    gzr,
    ag,
    fout,
    bsend,
    byr,
    bxs,
    bxr,
    bfin,
    lossz,
    lossx,
    lossc,
    lossv,
    load_sem,
    wsend_sem,
    wrecv_sem,
    psend_sem,
    precv_sem,
    ysend_sem,
    yrecv_sem,
    yrel_sem,
    xh_sem,
    st_sem,
    g_sem,
    agz_sem,
    agx_sem,
    agp_sem,
    b_sem,
    l_sem,
    out_sem,
):
    dp = lax.axis_index("dp")
    mp = lax.axis_index("mp")
    c = dp % 2
    z = (dp // 2) % NZ
    xl = dp // (2 * NZ)
    y = mp // 2
    xh = mp % 2

    pair = {"dp": dp + 1 - 2 * c}
    xpart = {"dp": (1 - xl) * 2 * NZ + z * 2 + c}
    xhpart = {"mp": y * 2 + 1 - xh}

    def at_z(zz):
        return {"dp": xl * 2 * NZ + zz * 2 + c}

    def at_mp(m):
        return {"mp": m}

    zup = at_z((z + 1) % NZ)
    yup = at_mp(((y + 1) % NY) * 2 + xh)
    ydown = at_mp(((y + NY - 1) % NY) * 2 + xh)
    zdown = at_z((z + NZ - 1) % NZ)

    def rcopy(src, dst, ssem, rsem, device):
        return pltpu.make_async_remote_copy(
            src_ref=src, dst_ref=dst, send_sem=ssem, recv_sem=rsem, device_id=device, device_id_type=MESH
        )

    barrier = pltpu.get_barrier_semaphore()
    peers = [pair, xpart]
    peers += [at_z((z + o) % NZ) for o in range(1, NZ)]
    peers += [at_mp((mp + o) % 8) for o in range(1, 8)]
    for device in peers:
        pl.semaphore_signal(barrier, inc=1, device_id=device, device_id_type=MESH)

    loads = [
        pltpu.make_async_copy(src, dst, load_sem.at[i])
        for i, (src, dst) in enumerate(
            (
                (w6_hbm, w6_in),
                (wg_hbm, wg_in),
                (h6_hbm, h6),
                (hg_hbm, hg),
                (stu_hbm, stu),
                (p6_hbm, pt.at[pl.ds(0, 400)]),
                (pg_hbm, pt.at[pl.ds(400, 176)]),
                (r6_hbm, r6),
                (rg_hbm, rg),
                (keep_hbm, keep),
            )
        )
    ]
    for load in loads[:2]:
        load.start()

    def slot_of(block):
        plane, off = block
        pl_ = xl if plane == 0 else 1 - xl
        return pl_ * 2 * NZ + ((z + off + NZ) % NZ) * 2

    def piece(p, slot):
        if p == 0:
            return gath6.at[slot, pl.ds(0, 80)]
        if p == 1:
            return gath6.at[slot, pl.ds(80, 32)]
        return gathg.at[slot]

    wtargets = (zup, zdown, xpart)
    pending = []

    def send_w(s, k, p):
        ref = piece(p, slot_of(SENDS[s][k]) + c)
        cp = rcopy(ref, ref, wsend_sem.at[p, 3 * s + k], wrecv_sem.at[p, 3 * s + k], wtargets[k])
        cp.start()
        pending.append(cp)

    def send_pair(unit, block, p):
        ref = piece(p, slot_of(block) + c)
        cp = rcopy(ref, ref, psend_sem.at[p, unit], precv_sem.at[p, unit], pair)
        cp.start()
        pending.append(cp)

    def wait_w(s, k, p):
        ref = piece(p, slot_of(RECVS[s][k]) + c)
        rcopy(ref, ref, wsend_sem.at[p, 3 * s + k], wrecv_sem.at[p, 3 * s + k], wtargets[k]).wait_recv()

    own = dp
    loads[0].wait()
    gath6[own, 96:112, :] = jnp.zeros((16, 1664), BF16)
    gath6[own, 0:96, 1536:1664] = jnp.zeros((96, 128), BF16)
    gath6[own, 0:100, 0:1600] = w6_in[...]
    pl.semaphore_wait(barrier, len(peers))
    for p in range(2):
        for k in range(3):
            send_w(0, k, p)
    loads[1].wait()
    wpad[0:4, :] = jnp.zeros((4, 768), F32)
    wpad[4:48, :] = wg_in[...].astype(F32)
    gathg[own] = wpad[...].astype(BF16)
    for k in range(3):
        send_w(0, k, 2)
    for p in range(3):
        send_pair(OWN, (0, 0), p)
    for load in loads[2:]:
        load.start()

    def column(row):
        a = lax.broadcasted_iota(jnp.int32, (112, 112), 0)
        b = lax.broadcasted_iota(jnp.int32, (112, 112), 1)
        return jnp.sum(jnp.where(a == b, row.astype(F32), 0.0), axis=1, keepdims=True)

    rows6[:, 1536:1664] = jnp.zeros((336, 128), BF16)
    def pick_rows(i):
        lane = lax.broadcasted_iota(jnp.int32, (112, 560), 1).astype(F32)
        pick = (column(keep[i : i + 1, :]) == lane).astype(F32).astype(BF16)
        rows6[112 * i : 112 * i + 112, 0:1600] = nn(pick, h6[i]).astype(BF16)
        rowsg[112 * i : 112 * i + 112, :] = nn(pick, hg[i]).astype(BF16)

    loads[2].wait()
    loads[3].wait()
    loads[9].wait()
    pick_rows(0)
    pick_rows(1)

    ysends = []
    relays = []

    SUBS = ((0, 80), (80, 64))

    def compute(items, sub):
        slots = [slot_of(block) for unit, block in items]
        for (unit, block), slot in zip(items, slots):
            for p in ((0,), (1, 2))[sub]:
                ref = piece(p, slot + 1 - c)
                rcopy(ref, ref, psend_sem.at[p, unit], precv_sem.at[p, unit], pair).wait_recv()

        def rows_of(ref, lo, hi):
            blocks = [ref[pl.ds(slot, 2), lo:hi].reshape(2 * (hi - lo), ref.shape[2]) for slot in slots]
            return jnp.concatenate(blocks, axis=0)

        if sub == 0:
            six = nt(rows_of(gath6, 0, 80), rows6[...]).astype(BF16)
            for i, slot in enumerate(slots):
                part[pl.ds(slot, 2), 0:80, :] = six[160 * i : 160 * i + 160].reshape(2, 80, 336)
        else:
            six = nt(rows_of(gath6, 80, 112), rows6[...])
            giant = nt(rows_of(gathg, 0, 48), rowsg[...])
            for i, slot in enumerate(slots):
                for cc in range(2):
                    a = six[64 * i + 32 * cc : 64 * i + 32 * cc + 32]
                    b = giant[96 * i + 48 * cc : 96 * i + 48 * cc + 48]
                    part[slot + cc, 80:96, :] = a[0:16].astype(BF16)
                    part[slot + cc, 96:112, :] = (a[16:32] + b[0:16]).astype(BF16)
                    part[slot + cc, 112:144, :] = b[16:48].astype(BF16)
        for (unit, block), slot in zip(items, slots):
            pass_round(unit, slot, sub)

    def pass_round(unit, slot, sub):
        lo, n = SUBS[sub]
        role = (y - slot // 8 + NY) % NY
        u = (slot // 2) % 4
        rows = pl.ds(lo, n)

        def send(cond, src, dst, ssem, rsem, device):
            @pl.when(cond)
            def _():
                rcopy(src, dst, ssem, rsem, device).start()

            ysends.append((cond, lambda: rcopy(src, dst, ssem, rsem, device)))

        first, second = part.at[slot, rows], part.at[slot + 1, rows]
        rel, rsem = yrel.at[unit, rows], yrel_sem.at[sub, unit]
        s0, s1 = ysend_sem.at[sub, unit, 0], ysend_sem.at[sub, unit, 1]
        send(role == 2, first, rel, s0, rsem, ydown)
        send(role == 2, second, rel, s1, rsem, yup)
        send(role == 1, second, yrecv.at[0, u, 1, rows], s0, yrecv_sem.at[sub, 0, u, 1], ydown)
        send(role == 3, first, yrecv.at[1, u, 0, rows], s0, yrecv_sem.at[sub, 1, u, 0], yup)

        def relay():
            for want, cc, side, device in ((1, 0, 0, ydown), (3, 1, 1, yup)):

                def descriptor(cc=cc, side=side, device=device):
                    dst = yrecv.at[side, u, cc, rows]
                    return rcopy(part.at[slot + cc, rows], dst, s1, yrecv_sem.at[sub, side, u, cc], device)

                @pl.when(role == want)
                def _(cc=cc, device=device, descriptor=descriptor):
                    rcopy(rel, rel, s1, rsem, device).wait_recv()
                    both = part[slot + cc, lo : lo + n].astype(F32) + yrel[unit, lo : lo + n].astype(F32)
                    part[slot + cc, lo : lo + n] = both.astype(BF16)
                    descriptor().start()

                ysends.append((role == want, descriptor))

        relays.append(relay)

    def head_out(i):
        if i == 0:
            for load in loads[4:9]:
                load.wait()
        outs[192 * i : 192 * i + 192, :] = nt(pt[192 * i : 192 * i + 192, :], stu[...])

    def turn_heads(lo, hi):
        for l in range(lo, hi):
            pmat[128 * l : 128 * l + 128, :] = pt[:, 128 * l : 128 * l + 128].T

    def residuals(i):
        row = jnp.concatenate([keep[j : j + 1, :] for j in range(3)], axis=1)
        pos = lax.broadcasted_iota(jnp.int32, (560, 336), 0)
        col = lax.broadcasted_iota(jnp.int32, (560, 336), 1)
        clip = (col >= 112 * i) & (col < 112 * i + 112)
        pick = ((row == pos) & clip).astype(F32).astype(BF16)
        a = nn(r6[i], pick)
        b = nn(rg[i], pick)
        if i == 0:
            tgt[0:400, :] = a
            tgt[400:576, :] = b
        else:
            tgt[0:400, :] += a
            tgt[400:576, :] += b

    work = [functools.partial(head_out, i) for i in range(3)]
    work += [functools.partial(residuals, i) for i in range(3)]
    work += [functools.partial(turn_heads, 0, 6), functools.partial(turn_heads, 6, 11)]

    def step_units(s):
        return [(3 * s + k, RECVS[s][k]) for k in range(3)]

    def run_relays(keep_back):
        while len(relays) > keep_back:
            relays.pop(0)()

    for s in range(STEPS):
        for ps in ((0,), (1, 2)):
            for p in ps:
                for k in range(3):
                    wait_w(s, k, p)
                if s + 1 < STEPS:
                    for k in range(3):
                        send_w(s + 1, k, p)
                for k in range(3):
                    send_pair(3 * s + k, RECVS[s][k], p)
            if ps == (0,):
                if s == 0:
                    pick_rows(2)
                    compute([(OWN, (0, 0))], 0)
                    compute([(OWN, (0, 0))], 1)
                else:
                    compute(step_units(s - 1), 1)
                run_relays(3)
                compute(step_units(s), 0)
            elif s + 1 < STEPS:
                work.pop(0)()
                work.pop(0)()
                run_relays(3)

    def summed(u, cc, sub):
        lo, n = SUBS[sub]
        total = part[y * 8 + u * 2 + cc, lo : lo + n].astype(F32)
        for side in range(2):
            total = total + yrecv[side, u, cc, lo : lo + n].astype(F32)
        return total

    def wait_y(u, sub):
        for side in range(2):
            for cc in range(2):
                ref = yrecv.at[side, u, cc, pl.ds(*SUBS[sub])]
                rcopy(ref, ref, ysend_sem.at[0, 0, 0], yrecv_sem.at[sub, side, u, cc], xhpart).wait_recv()

    def xh_copy(k, sub):
        rows = pl.ds(*SUBS[sub])
        src, dst = xsend.at[k, pl.ds(0, 2), rows], xrecv.at[k, pl.ds(0, 2), rows]
        return rcopy(src, dst, xh_sem.at[0, k, sub], xh_sem.at[1, k, sub], xhpart)

    def exchange(sub):
        lo, n = SUBS[sub]
        for k in range(2):
            u = 2 * (1 - xh) + k
            wait_y(u, sub)
            for cc in range(2):
                xsend[k, cc, lo : lo + n] = summed(u, cc, sub).astype(BF16)
            xh_copy(k, sub).start()

    def targets(sub):
        for k in range(2):
            u = 2 * xh + k
            wait_y(u, sub)
            xh_copy(k, sub).wait_recv()
            lo, n = SUBS[sub]
            for cc in range(2):
                total = summed(u, cc, sub) + xrecv[k, cc, lo : lo + n].astype(F32)
                f = 100 * (2 * k + cc)
                if sub == 0:
                    tgt[f : f + 80, :] += total
                else:
                    tgt[f + 80 : f + 100, :] += total[0:20]
                    f = 400 + 44 * (2 * k + cc)
                    tgt[f : f + 44, :] += total[20:64]

    early = y // 2 == xl

    run_relays(0)
    compute(step_units(STEPS - 1), 1)
    exchange(0)
    pl.when(early)(functools.partial(exchange, 1))
    run_relays(0)
    pl.when(jnp.logical_not(early))(functools.partial(exchange, 1))
    targets(0)
    targets(1)

    def sums(lo, hi):
        t = tgt[lo:hi, :]
        o = outs[lo:hi, :]
        return [
            jnp.sum(o * t, axis=0, keepdims=True),
            jnp.sum(o * o, axis=0, keepdims=True),
            jnp.sum(t * t, axis=0, keepdims=True),
        ]

    for i, row in enumerate(sums(0, 400) + sums(400, 576)):
        stats[mp, i : i + 1, :] = row
    for i in range(6, 8):
        stats[mp, i : i + 1, :] = jnp.zeros((1, 336), F32)
    st = []
    for o in range(1, 8):
        m = (mp + o) % 8
        cp = rcopy(stats.at[mp], stats.at[mp], st_sem.at[0, o], st_sem.at[1, mp], at_mp(m))
        cp.start()
        pending.append(cp)
    for o in range(1, 8):
        m = (mp + o) % 8
        rcopy(stats.at[m], stats.at[m], st_sem.at[0, o], st_sem.at[1, m], at_mp(m)).wait_recv()
    total = stats[0]
    for m in range(1, 8):
        total = total + stats[m]

    def gradient(lo, hi, i):
        norm_out = jnp.sqrt(total[i + 1 : i + 2] + norm_eps)
        norm_tar = jnp.sqrt(total[i + 2 : i + 3] + norm_eps)
        both = norm_out * norm_tar
        cosine = total[i : i + 1] / both
        a = -loss_scale / both
        b = loss_scale * cosine / (norm_out * norm_out)
        grad[lo:hi, :] = (tgt[lo:hi, :] * a + outs[lo:hi, :] * b).astype(BF16)
        return cosine

    cos6 = gradient(0, 400, 0)
    cosg = gradient(400, 576, 3)
    loss_local = jnp.sum(2.0 - cos6 - cosg, axis=1, keepdims=True)
    lossz[z] = jnp.broadcast_to(loss_local, (8, 128))
    for o in range(1, NZ):
        zz = (z + o) % NZ
        cp = rcopy(lossz.at[z], lossz.at[z], l_sem.at[0, o], l_sem.at[1, z], at_z(zz))
        cp.start()
        pending.append(cp)

    offsets = (-4, -3, 3, 1, -2, 2, -1, 0)
    at = {off: (z + off + NZ) % NZ for off in offsets}

    def head_rows(core):
        rows = grad[pl.ds(pl.multiple_of(core * 288, 16), 288), :]
        g = nn(rows, stu[...]).astype(BF16)
        for x in range(2):
            for r in range(9):
                for l in range(11):
                    t = r * 11 + l
                    lo = 144 * x + 16 * r
                    gs[t // 13, 2 * core + x, t % 13] = g[lo : lo + 16, 128 * l : 128 * l + 128]
            for j in range(8, 13):
                gs[7, 2 * core + x, j] = jnp.zeros((16, 128), BF16)

    head_rows(1 - c)
    for kk in at.values():
        cp = rcopy(gs.at[kk, pl.ds(2 * (1 - c), 2)], grecv.at[kk], g_sem.at[0, kk], g_sem.at[1, kk], pair)
        cp.start()
        pending.append(cp)
    head_rows(c)

    def both_cores(kk, x):
        return gs[kk, 2 * c + x].astype(F32) + grecv[kk, x].astype(F32)

    def to_x(kk):
        cp = rcopy(gxs.at[kk], gxr.at[kk], g_sem.at[2, kk], g_sem.at[3, kk], xpart)
        cp.start()
        pending.append(cp)

    def z_hop(src, sid, step):
        cp = rcopy(src, gzr.at[sid], g_sem.at[4, sid], g_sem.at[5, sid], at_z((z + step + NZ) % NZ))
        cp.start()
        pending.append(cp)

    def from_hop(sid):
        rcopy(gzr.at[sid], gzr.at[sid], g_sem.at[4, sid], g_sem.at[5, sid], pair).wait_recv()
        return gzr[sid].astype(F32)

    for off, kk in at.items():
        rcopy(grecv.at[kk], grecv.at[kk], g_sem.at[0, kk], g_sem.at[1, kk], pair).wait_recv()
        if off:
            gxs[kk] = both_cores(kk, 1 - xl).astype(BF16)
            if off == 1:
                z_hop(gxs.at[kk], 7, 1)
            else:
                to_x(kk)

    def back_pair(t):
        yy = (y + t) % NY
        rows = pmat[pl.ds(pl.multiple_of(yy * 352, 16), 352), :]
        bsend[yy] = nn(rows, grad[...]).astype(BF16).reshape(2, 176, 336)
        if t:
            o = (3 - t) % NY
            cp = rcopy(bsend.at[yy], byr.at[o], b_sem.at[0, t], b_sem.at[1, o], at_mp(yy * 2 + xh))
            cp.start()
            pending.append(cp)

    def own_part(off):
        kk = at[off]
        v = both_cores(kk, xl)
        if off != 1:
            rcopy(gxr.at[kk], gxr.at[kk], g_sem.at[2, kk], g_sem.at[3, kk], xpart).wait_recv()
            v = v + gxr[kk].astype(F32)
        return v

    def pass_on(off, value, sid, step):
        gzs[at[off]] = value.astype(BF16)
        z_hop(gzs.at[at[off]], sid, step)

    pass_on(1, own_part(1), 4, 1)
    back_pair(2)
    back_pair(1)
    gxs[z] = (both_cores(z, 1 - xl) + from_hop(7)).astype(BF16)
    to_x(z)
    pass_on(-4, own_part(-4), 0, -2)
    pass_on(-3, own_part(-3), 1, -1)
    pass_on(3, own_part(3), 2, 1)
    back_pair(3)
    back_pair(0)
    pass_on(-2, own_part(-2) + from_hop(0) + from_hop(1), 5, -2)
    pass_on(2, own_part(2) + from_hop(2), 6, 2)
    pass_on(-1, own_part(-1), 3, -1)

    for o in range(1, NZ):
        zz = (z + o) % NZ
        rcopy(lossz.at[zz], lossz.at[zz], l_sem.at[0, o], l_sem.at[1, zz], at_z(zz)).wait_recv()
    loss = lossz[0]
    for zz in range(1, NZ):
        loss = loss + lossz[zz]
    lossx[0] = loss
    cp = rcopy(lossx.at[0], lossx.at[1], l_sem.at[2, 0], l_sem.at[2, 1], xpart)
    cp.start()
    pending.append(cp)

    for o in range(3):
        rcopy(byr.at[o], byr.at[o], b_sem.at[0, 0], b_sem.at[1, o], xhpart).wait_recv()

    def back_sum(j):
        v = bsend[y, j].astype(F32)
        for o in range(3):
            v = v + byr[o, j].astype(F32)
        return v

    bxs[...] = back_sum(1 - xh).astype(BF16)
    bcp = rcopy(bxs, bxr, b_sem.at[2, 0], b_sem.at[2, 1], xhpart)
    bcp.start()
    pending.append(bcp)

    total = own_part(0)
    for sid in (4, 3, 6, 5):
        total = total + from_hop(sid)
    q_own = 2 * c + xl
    q_x = 2 * c + 1 - xl
    ag[z, q_own] = (total * (head_scale / token_total)).astype(BF16)

    def ag_send(ref, ssem, rsem, device):
        cp = rcopy(ref, ref, ssem, rsem, device)
        cp.start()
        pending.append(cp)

    def ag_z(ref, sid, rsem, off):
        ag_send(ref, agz_sem.at[0, sid], rsem, at_z((z + off + NZ) % NZ))

    mine = ag.at[z, q_own]
    ag_z(mine, 0, agz_sem.at[1, z], 1)
    ag_z(mine, 1, agz_sem.at[1, z], -1)
    ag_send(mine, agx_sem.at[0, z], agx_sem.at[1, z], xpart)
    ag_z(mine, 2, agz_sem.at[1, z], 2)
    ag_z(mine, 3, agz_sem.at[1, z], -2)
    ag_send(mine, agp_sem.at[0, z, xl], agp_sem.at[1, z, xl], pair)

    def from_z(off):
        zz = (z + off + NZ) % NZ
        ref = ag.at[zz, q_own]
        rcopy(ref, ref, agz_sem.at[0, 0], agz_sem.at[1, zz], pair).wait_recv()
        if off == -2:
            ag_z(ref, 4, agz_sem.at[1, zz], 2)
            ag_z(ref, 5, agz_sem.at[1, zz], 1)
        if off == 2:
            ag_z(ref, 6, agz_sem.at[1, zz], -1)
        if off != 1:
            ag_send(ref, agx_sem.at[0, zz], agx_sem.at[1, zz], xpart)
        ag_send(ref, agp_sem.at[0, zz, xl], agp_sem.at[1, zz, xl], pair)

    def from_x(off):
        zz = (z + off + NZ) % NZ
        ref = ag.at[zz, q_x]
        rcopy(ref, ref, agx_sem.at[0, zz], agx_sem.at[1, zz], xpart).wait_recv()
        if off == 0:
            ag_z(ref, 7, agx_sem.at[1, zz], -1)
        ag_send(ref, agp_sem.at[0, zz, 1 - xl], agp_sem.at[1, zz, 1 - xl], pair)

    from_z(-1)
    from_z(1)
    from_x(0)
    from_z(-2)
    from_z(2)

    rcopy(lossx.at[0], lossx.at[1], l_sem.at[2, 0], l_sem.at[2, 1], xpart).wait_recv()
    lossc[0] = lossx[0] + lossx[1]
    cp = rcopy(lossc.at[0], lossc.at[1], l_sem.at[3, 0], l_sem.at[3, 1], pair)
    cp.start()
    pending.append(cp)
    bcp.wait_recv()
    v = back_sum(xh) + bxr[...].astype(F32)
    for i in range(3):
        bfin[i] = v[:, 112 * i : 112 * i + 112]
    back_store = pltpu.make_async_copy(bfin, back_out, out_sem.at[2])
    back_store.start()

    from_x(-1)
    from_z(-3)
    from_z(3)
    rcopy(lossc.at[0], lossc.at[1], l_sem.at[3, 0], l_sem.at[3, 1], pair).wait_recv()
    lossv[...] = (lossc[0, 0:1, 0:1] + lossc[1, 0:1, 0:1]) / token_total
    loss_store = pltpu.make_async_copy(lossv, loss_out, out_sem.at[3])
    loss_store.start()
    from_x(1)
    from_z(-4)
    for off in (-2, 2, -3, 3, -4):
        from_x(off)

    def lay_out(zz, core):
        for x in range(2):
            for j in range(13 if zz < 7 else 8):
                r, l = divmod(zz * 13 + j, 11)
                rows = pl.ds(pl.multiple_of(288 * core + (144 * x + 16 * r), 16), 16)
                fout[rows, 128 * l : 128 * l + 128] = ag[zz, 2 * core + x, j]

    for zz in range(NZ):
        lay_out(zz, c)
    for zz in range(NZ):
        for x in range(2):
            ref = ag.at[zz, 2 * (1 - c) + x]
            rcopy(ref, ref, agp_sem.at[0, zz, x], agp_sem.at[1, zz, x], pair).wait_recv()
        lay_out(zz, 1 - c)
    stores = [
        back_store,
        loss_store,
        pltpu.make_async_copy(fout.at[pl.ds(0, 400)], gp6_out, out_sem.at[0]),
        pltpu.make_async_copy(fout.at[pl.ds(400, 176)], gpg_out, out_sem.at[1]),
    ]
    stores[2].start()
    stores[3].start()

    for away, descriptor in ysends:

        @pl.when(away)
        def _(descriptor=descriptor):
            descriptor().wait_send()

    for k in range(2):
        for sub in range(2):
            xh_copy(k, sub).wait_send()
    for cp in pending:
        cp.wait_send()
    for cp in stores:
        cp.wait()


def local(
    student_feats,
    keep_index,
    hidden_six,
    resid_six,
    down_six,
    hidden_giant,
    resid_giant,
    down_giant,
    proj_six,
    proj_giant,
):
    token_total = 336 * 32
    dma = pltpu.SemaphoreType.DMA
    hbm = pl.BlockSpec(memory_space=pl.ANY)
    scratch = [
        pltpu.VMEM((3, 112), jnp.int32),
        pltpu.VMEM((100, 1600), BF16),
        pltpu.VMEM((44, 768), BF16),
        pltpu.VMEM((32, 112, 1664), BF16),
        pltpu.VMEM((32, 48, 768), BF16),
        pltpu.VMEM((3, 560, 1600), BF16),
        pltpu.VMEM((3, 560, 768), BF16),
        pltpu.VMEM((3, 400, 560), BF16),
        pltpu.VMEM((3, 176, 560), BF16),
        pltpu.VMEM((336, 1664), BF16),
        pltpu.VMEM((336, 768), BF16),
        pltpu.VMEM((336, 1408), BF16),
        pltpu.VMEM((576, 1408), BF16),
        pltpu.VMEM((1408, 576), BF16),
        pltpu.VMEM((32, 144, 336), BF16),
        pltpu.VMEM((2, 4, 2, 144, 336), BF16),
        pltpu.VMEM((2, 2, 144, 336), BF16),
        pltpu.VMEM((2, 2, 144, 336), BF16),
        pltpu.VMEM((48, 768), F32),
        pltpu.VMEM((16, 144, 336), BF16),
        pltpu.VMEM((576, 336), F32),
        pltpu.VMEM((576, 336), F32),
        pltpu.VMEM((8, 8, 336), F32),
        pltpu.VMEM((576, 336), BF16),
        pltpu.VMEM((NZ, 4, 13, 16, 128), BF16),
        pltpu.VMEM((NZ, 2, 13, 16, 128), BF16),
        pltpu.VMEM((NZ, 13, 16, 128), BF16),
        pltpu.VMEM((NZ, 13, 16, 128), BF16),
        pltpu.VMEM((NZ, 13, 16, 128), BF16),
        pltpu.VMEM((NZ, 13, 16, 128), BF16),
        pltpu.VMEM((NZ, 4, 13, 16, 128), BF16),
        pltpu.VMEM((576, 1408), BF16),
        pltpu.VMEM((NY, 2, 176, 336), BF16),
        pltpu.VMEM((3, 2, 176, 336), BF16),
        pltpu.VMEM((176, 336), BF16),
        pltpu.VMEM((176, 336), BF16),
        pltpu.VMEM((3, 176, 112), F32),
        pltpu.VMEM((NZ, 8, 128), F32),
        pltpu.VMEM((2, 8, 128), F32),
        pltpu.VMEM((2, 8, 128), F32),
        pltpu.VMEM((1, 1), F32),
        dma((10,)),
        dma((3, 15)),
        dma((3, 15)),
        dma((3, 16)),
        dma((3, 16)),
        dma((2, 16, 2)),
        dma((2, 2, 4, 2)),
        dma((2, 16)),
        dma((2, 2, 2)),
        dma((2, 8)),
        dma((6, 8)),
        dma((3, 8)),
        dma((2, 8)),
        dma((2, 8, 2)),
        dma((3, 4)),
        dma((4, 8)),
        dma((4,)),
    ]
    gp6, gpg, back, loss = pl.pallas_call(
        functools.partial(kernel, token_total),
        out_shape=(
            jax.ShapeDtypeStruct((400, 1408), BF16),
            jax.ShapeDtypeStruct((176, 1408), BF16),
            jax.ShapeDtypeStruct((3, 176, 112), F32),
            jax.ShapeDtypeStruct((1, 1), F32),
        ),
        in_specs=[hbm] * 10,
        out_specs=(hbm, hbm, hbm, hbm),
        scratch_shapes=scratch,
        compiler_params=pltpu.CompilerParams(
            collective_id=0, has_side_effects=True, vmem_limit_bytes=62 * 1024 * 1024
        ),
        cost_estimate=pl.CostEstimate(flops=6_000_000_000, bytes_accessed=20_000_000, transcendentals=0),
    )(
        keep_index,
        student_feats.reshape(336, 1408),
        hidden_six,
        resid_six.transpose(0, 2, 1),
        down_six.T,
        hidden_giant,
        resid_giant.transpose(0, 2, 1),
        down_giant.T,
        proj_six.T,
        proj_giant.T,
    )
    return (back.transpose(0, 2, 1), gp6.astype(F32).T, gpg.astype(F32).T, loss.reshape(()))


def solution(mesh):
    return jax.shard_map(
        local,
        mesh=mesh,
        in_specs=(
            P("dp", None, None),
            P("dp", None),
            P("dp", None, "mp"),
            P("dp", None, "mp"),
            P("mp", "dp"),
            P("dp", None, "mp"),
            P("dp", None, "mp"),
            P("mp", "dp"),
            P(None, "mp"),
            P(None, "mp"),
        ),
        out_specs=(P("dp", None, "mp"), P(None, "mp"), P(None, "mp"), P()),
        check_vma=False,
    )
```
